512 devices in a mesh: ctx: 64 (over y, z), head: 8 (over x, core).
Axes of the slice: x: 4, y: 4, z: 16, core: 2. Of those that a mesh axis runs over, the one named last changes fastest.
Arguments:
- queries: bfloat16 [2, 8, 128, 576], P(None, None, 'head')
- cache: bfloat16 [8, 16384, 576], P(None, 'ctx')
- lengths: int32 [8], replicated, may hold values from 4096 to 16384, as said below
- positions: int32 [8], replicated, may hold values from 0 to 16383, as said below
- up_weight: bfloat16 [128, 128, 512], P('head', 'ctx'), may hold values from -2 to 2
- out_weight: bfloat16 [128, 128, 7168], P('head', 'ctx'), may hold values from -0.0625 to 0.0625
Outputs:
- attended: bfloat16 [2, 8, 7168], P(None, None, 'head')
The draws below stay inside these ranges and needn't reach their ends.
Inputs may be any that keep to these rules, and one draw needn't show every extreme that they name: `lengths`: one sequence has exactly 16384. `positions`: one sequence has exactly 16383.
All inputs are finite; a program needn't handle non-finite values.
Results may differ from the reference program's by a relative error of at most 0.012.
Values may be sent and summed in bfloat16 or wider, within the bound.
No kernel may reach another device: no remote copies, remote signals or barrier semaphores. Data moves between devices by JAX's collectives and lax.ppermute only.
A program may use at most 128 MiB of HBM per device.

```python
import math
import jax
import jax.numpy as jnp
from jax import lax

LAT = 512
ROPE = 64
HEADS = 128
VDIM = 128
D = 7168
STEPS = 2
SEQS = 8
CTX = 16384


def latent_cache_entries(key):
    return jax.random.normal(key, (SEQS, CTX, LAT + ROPE), jnp.float32)


def draw_cache(key, part):
    return latent_cache_entries(key).astype(jnp.bfloat16)


def draw_queries(key, part):
    cached = latent_cache_entries(key)
    key = jax.random.fold_in(key, 2)
    base_key, pick_key, first_key, second_key, level_key, spacing_key, forced_key = jax.random.split(key, 7)
    shape = (STEPS, SEQS, HEADS, LAT + ROPE)
    entries = 1.5 * jax.random.normal(base_key, shape, jnp.float32)
    forced = jax.random.randint(forced_key, (SEQS,), 0, HEADS)
    picked = (jax.random.randint(pick_key, (SEQS, HEADS), 0, 4) == 0) | (jnp.arange(HEADS, dtype=jnp.int32)[None, :] == forced[:, None])
    first = jax.random.randint(first_key, (SEQS, HEADS), 0, CTX // 4 - 1)
    second = (first + 1 + jax.random.randint(second_key, (SEQS, HEADS), 0, CTX // 4 - 2)) % (CTX // 4 - 1)
    level = jax.random.uniform(level_key, (SEQS, HEADS), jnp.float32, 110.0, 320.0)
    spacing = jax.random.uniform(spacing_key, (SEQS, HEADS), jnp.float32, 1.0, 3.0)
    row_one = jnp.take_along_axis(cached, first[:, :, None], axis=1)[..., :LAT]
    row_two = jnp.take_along_axis(cached, second[:, :, None], axis=1)[..., :LAT]
    inv_scale = 192.0 ** 0.5
    aa = jnp.sum(row_one * row_one, axis=-1)
    bb = jnp.sum(row_two * row_two, axis=-1)
    ab = jnp.sum(row_one * row_two, axis=-1)
    want_one = level * inv_scale
    want_two = (level - spacing) * inv_scale
    determinant = aa * bb - ab * ab
    coef_one = (want_one * bb - want_two * ab) / determinant
    coef_two = (want_two * aa - want_one * ab) / determinant
    aligned = coef_one[..., None] * row_one + coef_two[..., None] * row_two
    latent_part = jnp.where(picked[None, :, :, None], aligned[None] + 0.02 * entries[..., :LAT], entries[..., :LAT])
    values = jnp.concatenate([latent_part, entries[..., LAT:]], axis=-1)
    return values.astype(jnp.bfloat16)


def draw_lengths(key, part):
    key = jax.random.fold_in(key, 3)
    draw_key, top_key = jax.random.split(key)
    drawn = jax.random.randint(draw_key, (SEQS,), CTX // 4, CTX + 1)
    longest = jax.random.randint(top_key, (), 0, SEQS)
    return jnp.where(jnp.arange(SEQS, dtype=jnp.int32) == longest, CTX, drawn).astype(jnp.int32)


def draw_positions(key, part):
    key = jax.random.fold_in(key, 4)
    draw_key, last_key = jax.random.split(key)
    drawn = jax.random.randint(draw_key, (SEQS,), 0, CTX)
    latest = jax.random.randint(last_key, (), 0, SEQS)
    return jnp.where(jnp.arange(SEQS, dtype=jnp.int32) == latest, CTX - 1, drawn).astype(jnp.int32)


def strengthened(array, rng, source, target, shards_of, factor):
    def block_of(position):
        return (jnp.arange(array.shape[position]) // (array.shape[position] // shards_of)).reshape((-1,) + (1,) * (array.ndim - 1 - position))

    one_side = jax.random.permutation(rng, shards_of)[block_of(target)]
    far = (block_of(target) + shards_of // 2) % shards_of
    return jnp.where((block_of(source) == one_side) | (block_of(source) == far), factor * array, array)


def block_scale(key, dims, pieces, low, largest):
    def one(position, blocks):
        heights = jax.random.uniform(jax.random.fold_in(jax.random.fold_in(key, 6), position), (blocks,), jnp.float32, low / len(pieces), largest / len(pieces))
        return jnp.repeat(jnp.exp(heights), dims[position] // blocks).reshape((-1,) + (1,) * (len(dims) - position - 1))

    factor_of = one(*pieces[0])
    for cut in pieces[1:]:
        factor_of = factor_of * one(*cut)
    return factor_of


def gaussian(rng, shape, deviation, most, shards=(), kind=jnp.bfloat16):
    values = deviation * jax.random.normal(rng, shape, jnp.float32)
    if shards:
        values = values * block_scale(rng, shape, shards, -0.22, 0.18)
    return jnp.clip(values, -most, most).astype(kind)


def heavy_noise(stream_key, dims, deviation, bound, shards, heavy, kind=jnp.bfloat16):
    entries = deviation * jax.random.normal(stream_key, dims, jnp.float32)
    if shards:
        entries = entries * block_scale(stream_key, dims, shards, -0.22, 0.18)
    return jnp.clip(strengthened(entries, jax.random.fold_in(stream_key, 3), *heavy), -bound, bound).astype(kind)


def setup_inputs(seed: int = 0) -> dict:
    key_of = jax.random.split(jax.random.key(seed), 7)
    queries = draw_queries(jax.random.fold_in(key_of[6], 71), 0)
    cache = draw_cache(jax.random.fold_in(key_of[6], 71), 0)
    lengths = draw_lengths(jax.random.fold_in(key_of[6], 71), 0)
    positions = draw_positions(jax.random.fold_in(key_of[6], 71), 0)
    up_weight = gaussian(key_of[4], (HEADS, VDIM, LAT), (LAT // 64) ** -0.5, 2.0, ((0, 8), (1, 64)))
    out_weight = heavy_noise(key_of[5], (HEADS, VDIM, D), (HEADS * VDIM) ** -0.5, 0.0625, ((0, 8), (1, 64)), (0, 2, 8, 2.0))
    return dict(queries=queries, cache=cache, lengths=lengths, positions=positions, up_weight=up_weight, out_weight=out_weight)


score_scale = 192.0 ** -0.5


def rotate(values, angle_pos):
    half = values.shape[-1] // 2
    freqs = jnp.exp(-jnp.arange(half, dtype=jnp.float32) * (2.0 / values.shape[-1]) * math.log(10000.0))
    angles = angle_pos[..., None] * freqs
    cosine = jnp.cos(angles)
    sine = jnp.sin(angles)
    first = values[..., :half]
    second = values[..., half:]
    return jnp.concatenate([first * cosine - second * sine, first * sine + second * cosine], axis=-1)


def reference(queries, cache, lengths, positions, up_weight, out_weight):
    floats = queries.astype(jnp.float32)
    decode_step_position = (positions[None, :] + jnp.arange(STEPS, dtype=jnp.int32)[:, None]).astype(jnp.float32)[:, :, None]
    rotated = jnp.concatenate([floats[..., :LAT], rotate(floats[..., LAT:], decode_step_position)], axis=-1).astype(jnp.bfloat16)
    by_seq = jnp.transpose(rotated, (1, 0, 2, 3))

    def one_sequence(packed):
        query_matrix_rows, cached, length = packed
        rows = query_matrix_rows.reshape(STEPS * HEADS, LAT + ROPE)
        scores = jnp.dot(rows, cached.T, preferred_element_type=jnp.float32).reshape(STEPS, HEADS, CTX) * score_scale
        limit = length - 1 + jnp.arange(STEPS, dtype=jnp.int32)
        valid = jnp.arange(CTX, dtype=jnp.int32)[None, None, :] < limit[:, None, None]
        top = jnp.max(jnp.where(valid, scores, -jnp.inf), axis=-1, keepdims=True)
        attention_weight = jnp.where(valid, jnp.exp(jnp.where(valid, scores, top) - top), 0.0)
        total = jnp.sum(attention_weight, axis=-1)
        reduced_total = jnp.dot(attention_weight.astype(jnp.bfloat16).reshape(STEPS * HEADS, CTX), cached[:, :LAT],
                         preferred_element_type=jnp.float32).reshape(STEPS, HEADS, LAT)
        return (reduced_total / total[..., None]).astype(jnp.bfloat16)

    latent_vector = lax.map(one_sequence, (by_seq, cache, lengths))
    latent_vector = jnp.transpose(latent_vector, (1, 0, 2, 3))
    values = jnp.einsum('sbhl,hvl->sbhv', latent_vector.astype(jnp.float32), up_weight.astype(jnp.float32)).astype(jnp.bfloat16)
    flat = values.reshape(STEPS * SEQS, HEADS * VDIM)
    attended = jnp.dot(flat, out_weight.reshape(HEADS * VDIM, D), preferred_element_type=jnp.float32)
    return attended.reshape(STEPS, SEQS, D).astype(jnp.bfloat16)
```

```python
import math

import jax
import jax.numpy as jnp
from jax import lax
from jax.sharding import Mesh
from jax.sharding import PartitionSpec as P

LAT = 512
ROPE = 64
NY = 4
NZ = 16
LANES = 128

CONTEXT = ("y", "z")
HEAD = ("x", "c")
PLANE = ("y", "x", "c")

score_scale = 192.0 ** (-0.5)
neg_large = -1e30


def rotate(values, angle_pos):
    half = values.shape[-1] // 2
    freqs = jnp.exp(
        -jnp.arange(half, dtype=jnp.float32) * (2.0 / values.shape[-1]) * math.log(10000.0)
    )
    angles = angle_pos[..., None] * freqs
    cosine = jnp.cos(angles)
    sine = jnp.sin(angles)
    first = values[..., :half]
    second = values[..., half:]
    return jnp.concatenate(
        [first * cosine - second * sine, first * sine + second * cosine], axis=-1
    )


def exchange(array, axes):
    return lax.all_to_all(array, axes, 0, 0, tiled=True)


def gather(array, axis, size):
    return exchange(jnp.broadcast_to(array[None], (size,) + array.shape), axis)


def by_head(weights):
    me = lax.axis_index("z")
    held = [lax.dynamic_index_in_dim(weights, me, 0, keepdims=False)]
    for shift in range(1, NZ):
        block = lax.dynamic_index_in_dim(weights, (me + shift) % NZ, 0, keepdims=False)
        held.append(lax.ppermute(block, "z", [(i, (i + shift) % NZ) for i in range(NZ)]))
    return jnp.concatenate(held, axis=0)


def partial_attention(queries, cache, lengths, positions):
    steps, seqs, heads_dev, _ = queries.shape
    ctx_dev = cache.shape[1]
    floats = queries.astype(jnp.float32)
    decode_step_position = (
        positions[None, :] + jnp.arange(steps, dtype=jnp.int32)[:, None]
    ).astype(jnp.float32)[:, :, None]
    rotated = jnp.concatenate(
        [floats[..., :LAT], rotate(floats[..., LAT:], decode_step_position)], axis=-1
    ).astype(jnp.bfloat16)
    rows = jnp.transpose(rotated, (1, 0, 2, 3)).reshape(seqs, steps * heads_dev, LAT + ROPE)
    scores = (
        jnp.einsum("eic,ezc->eiz", rows, cache, preferred_element_type=jnp.float32) * score_scale
    )
    scores = scores.reshape(seqs, steps, heads_dev, ctx_dev)
    places = lax.axis_index(CONTEXT) * ctx_dev + jnp.arange(ctx_dev, dtype=jnp.int32)
    limit = lengths[:, None] - 1 + jnp.arange(steps, dtype=jnp.int32)[None, :]
    valid = places[None, None, None, :] < limit[:, :, None, None]
    masked = jnp.where(valid, scores, neg_large)
    top = jnp.max(masked, axis=-1)
    weight = jnp.where(valid, jnp.exp(masked - top[..., None]), 0.0)
    total = jnp.sum(weight, axis=-1)
    weight_rows = weight.astype(jnp.bfloat16).reshape(seqs, steps * heads_dev, ctx_dev)
    sums = jnp.einsum(
        "bqj,bjl->bql", weight_rows, cache[:, :, :LAT], preferred_element_type=jnp.float32
    ).reshape(seqs, steps, heads_dev, LAT)
    live = total > 0.0
    total = jnp.where(live, total, 1.0)
    level = jnp.where(live, top + jnp.log(total), neg_large)
    return sums / total[..., None], level


def in_parts(level):
    high = lax.reduce_precision(level, 8, 7)
    rest = level - high
    middle = lax.reduce_precision(rest, 8, 7)
    return high, middle, rest - middle


def local(queries, cache, lengths, positions, up_weight, out_weight):
    steps, seqs, heads_dev, _ = queries.shape
    width = out_weight.shape[2]
    groups = width // (width // 8)
    weights = by_head(jnp.concatenate([up_weight, out_weight], axis=-1))

    latents, level = partial_attention(queries, cache, lengths, positions)
    parts = jnp.stack(in_parts(level), axis=-1)
    parts = jnp.pad(parts, ((0, 0), (0, 0), (0, 0), (0, LANES - 3)))
    packet = jnp.concatenate([latents, parts], axis=-1).astype(jnp.bfloat16)
    pair = seqs // NY
    rows = pair * steps
    packet = packet.reshape(NY, pair, steps, heads_dev, LAT + LANES)
    packet = jnp.transpose(packet, (0, 3, 1, 2, 4)).reshape(NY * NZ, rows, LAT + LANES)
    came = exchange(packet, CONTEXT).astype(jnp.float32)
    levels = came[..., LAT] + came[..., LAT + 1] + came[..., LAT + 2]
    share = jnp.exp(levels - jnp.max(levels, axis=0, keepdims=True))
    share = share / jnp.sum(share, axis=0, keepdims=True)
    latent = jnp.sum(came[..., :LAT] * share[..., None], axis=0).astype(jnp.bfloat16)
    latent = gather(latent, "y", NY).reshape(NY * rows, LAT)

    values = jnp.einsum(
        "rl,vl->rv", latent, weights[:, :LAT], preferred_element_type=jnp.float32
    ).astype(jnp.bfloat16)
    partial = jnp.einsum(
        "rv,vd->rd", values, weights[:, LAT:], preferred_element_type=jnp.float32
    ).astype(jnp.bfloat16)
    partial = partial.reshape(NY, rows, groups, width // groups)
    partial = jnp.transpose(partial, (0, 2, 1, 3)).reshape(NY * groups, rows, width // groups)
    mine = jnp.sum(exchange(partial, PLANE).astype(jnp.float32), axis=0).astype(jnp.bfloat16)
    mine = jnp.sum(gather(mine, "z", NZ).astype(jnp.float32), axis=0).astype(jnp.bfloat16)
    whole = gather(mine, "y", NY).reshape(seqs, steps, width // groups)
    return jnp.transpose(whole, (1, 0, 2))


def solution(mesh):
    split = Mesh(mesh.devices.reshape(NY, NZ, -1, 2), ("y", "z", "x", "c"))
    return jax.shard_map(
        local,
        mesh=split,
        in_specs=(
            P(None, None, HEAD, None),
            P(None, CONTEXT, None),
            P(),
            P(),
            P(HEAD, CONTEXT, None),
            P(HEAD, CONTEXT, None),
        ),
        out_specs=P(None, None, HEAD),
        check_vma=False,
    )
```

```python
import math

import jax
import jax.numpy as jnp
from jax import lax
from jax.sharding import Mesh
from jax.sharding import PartitionSpec as P

LAT = 512
ROPE = 64
NY = 4
NB = 4
NL = 4
NZ = NB * NL
LANES = 128

CONTEXT = ("y", "b", "l")
ROW = ("b", "l")
NEAR = ("y", "l")
HEAD = ("x", "c")
PLANE = ("y", "x", "c")

score_scale = 192.0 ** (-0.5)
neg_large = -1e30


def rotate(values, angle_pos):
    half = values.shape[-1] // 2
    freqs = jnp.exp(
        -jnp.arange(half, dtype=jnp.float32) * (2.0 / values.shape[-1]) * math.log(10000.0)
    )
    angles = angle_pos[..., None] * freqs
    cosine = jnp.cos(angles)
    sine = jnp.sin(angles)
    first = values[..., :half]
    second = values[..., half:]
    return jnp.concatenate(
        [first * cosine - second * sine, first * sine + second * cosine], axis=-1
    )


def exchange(array, axes):
    return lax.all_to_all(array, axes, 0, 0, tiled=True)


def gather(array, axis, size):
    return exchange(jnp.broadcast_to(array[None], (size,) + array.shape), axis)


def by_heads(weights):
    me = lax.axis_index("b")
    blocks = weights.reshape((NB, -1) + weights.shape[1:])
    held = [lax.dynamic_index_in_dim(blocks, me, 0, keepdims=False)]
    for shift in range(1, NB):
        block = lax.dynamic_index_in_dim(blocks, (me + shift) % NB, 0, keepdims=False)
        held.append(lax.ppermute(block, "b", [(i, (i + shift) % NB) for i in range(NB)]))
    return jnp.stack(held, axis=0)


def partial_attention(queries, cache, lengths, positions):
    steps, seqs, heads_dev, _ = queries.shape
    ctx_dev = cache.shape[1]
    floats = queries.astype(jnp.float32)
    decode_step_position = (
        positions[None, :] + jnp.arange(steps, dtype=jnp.int32)[:, None]
    ).astype(jnp.float32)[:, :, None]
    rotated = jnp.concatenate(
        [floats[..., :LAT], rotate(floats[..., LAT:], decode_step_position)], axis=-1
    ).astype(jnp.bfloat16)
    rows = jnp.transpose(rotated, (1, 0, 2, 3)).reshape(seqs, steps * heads_dev, LAT + ROPE)
    scores = (
        jnp.einsum("eic,ezc->eiz", rows, cache, preferred_element_type=jnp.float32) * score_scale
    )
    scores = scores.reshape(seqs, steps, heads_dev, ctx_dev)
    places = lax.axis_index(CONTEXT) * ctx_dev + jnp.arange(ctx_dev, dtype=jnp.int32)
    limit = lengths[:, None] - 1 + jnp.arange(steps, dtype=jnp.int32)[None, :]
    valid = places[None, None, None, :] < limit[:, :, None, None]
    masked = jnp.where(valid, scores, neg_large)
    top = jnp.max(masked, axis=-1)
    weight = jnp.where(valid, jnp.exp(masked - top[..., None]), 0.0)
    total = jnp.sum(weight, axis=-1)
    weight_rows = weight.astype(jnp.bfloat16).reshape(seqs, steps * heads_dev, ctx_dev)
    sums = jnp.einsum(
        "bqj,bjl->bql", weight_rows, cache[:, :, :LAT], preferred_element_type=jnp.float32
    ).reshape(seqs, steps, heads_dev, LAT)
    live = total > 0.0
    total = jnp.where(live, total, 1.0)
    level = jnp.where(live, top + jnp.log(total), neg_large)
    return sums / total[..., None], level


def in_parts(level):
    high = lax.reduce_precision(level, 8, 7)
    rest = level - high
    middle = lax.reduce_precision(rest, 8, 7)
    return high, middle, rest - middle


def local(queries, cache, lengths, positions, up_weight, out_weight):
    steps, seqs, heads_dev, _ = queries.shape
    width = out_weight.shape[2]
    groups = width // (width // 8)
    weights = by_heads(jnp.concatenate([up_weight, out_weight], axis=-1))

    latents, level = partial_attention(queries, cache, lengths, positions)
    parts = jnp.stack(in_parts(level), axis=-1)
    parts = jnp.pad(parts, ((0, 0), (0, 0), (0, 0), (0, LANES - 3)))
    packet = jnp.concatenate([latents, parts], axis=-1).astype(jnp.bfloat16)
    pair = seqs // NY
    rows = pair * steps
    packet = packet.reshape(NY, pair, steps, heads_dev, LAT + LANES)
    packet = jnp.transpose(packet, (0, 3, 1, 2, 4)).reshape(NY * NZ, rows, LAT + LANES)
    came, weights = lax.optimization_barrier((exchange(packet, CONTEXT), weights))
    came = came.astype(jnp.float32)
    levels = came[..., LAT] + came[..., LAT + 1] + came[..., LAT + 2]
    share = jnp.exp(levels - jnp.max(levels, axis=0, keepdims=True))
    share = share / jnp.sum(share, axis=0, keepdims=True)
    latent = jnp.sum(came[..., :LAT] * share[..., None], axis=0).astype(jnp.bfloat16)
    latent = gather(latent, NEAR, NY * NL).reshape(NY, NL, rows, LAT)

    values = jnp.einsum(
        "yhrl,shvl->yrshv", latent, weights[..., :LAT], preferred_element_type=jnp.float32
    ).astype(jnp.bfloat16)
    partial = jnp.einsum(
        "yrshv,shvd->yrd", values, weights[..., LAT:], preferred_element_type=jnp.float32
    ).astype(jnp.bfloat16)
    partial = partial.reshape(NY, rows, groups, width // groups)
    partial = jnp.transpose(partial, (0, 2, 1, 3)).reshape(NY * groups, rows, width // groups)
    mine = jnp.sum(exchange(partial, PLANE).astype(jnp.float32), axis=0).astype(jnp.bfloat16)
    mine = jnp.sum(gather(mine, ROW, NZ).astype(jnp.float32), axis=0).astype(jnp.bfloat16)
    whole = gather(mine, "y", NY).reshape(seqs, steps, width // groups)
    return jnp.transpose(whole, (1, 0, 2))


def solution(mesh):
    split = Mesh(mesh.devices.reshape(NY, NB, NL, -1, 2), ("y", "b", "l", "x", "c"))
    return jax.shard_map(
        local,
        mesh=split,
        in_specs=(
            P(None, None, HEAD, None),
            P(None, CONTEXT, None),
            P(),
            P(),
            P(HEAD, CONTEXT, None),
            P(HEAD, CONTEXT, None),
        ),
        out_specs=P(None, None, HEAD),
        check_vma=False,
    )
```

```python
import math

import jax
import jax.numpy as jnp
from jax import lax
from jax.sharding import Mesh
from jax.sharding import PartitionSpec as P

LAT = 512
ROPE = 64
NY = 4
NZ = 16
LANES = 128

CONTEXT = ("y", "z")
HEAD = ("x", "c")

score_scale = 192.0 ** (-0.5)
neg_large = -1e30


def rotate(values, angle_pos):
    half = values.shape[-1] // 2
    freqs = jnp.exp(
        -jnp.arange(half, dtype=jnp.float32) * (2.0 / values.shape[-1]) * math.log(10000.0)
    )
    angles = angle_pos[..., None] * freqs
    cosine = jnp.cos(angles)
    sine = jnp.sin(angles)
    first = values[..., :half]
    second = values[..., half:]
    return jnp.concatenate(
        [first * cosine - second * sine, first * sine + second * cosine], axis=-1
    )


def exchange(array, axes):
    return lax.all_to_all(array, axes, 0, 0, tiled=True)


def gather(array, axis, size):
    return exchange(jnp.broadcast_to(array[None], (size,) + array.shape), axis)


def of_columns(up_weight, out_weight, groups):
    both = lax.all_gather(jnp.concatenate([up_weight, out_weight], axis=-1), "y")
    block = out_weight.shape[2] // groups
    part = block // NY
    rest = both[..., LAT:].reshape(both.shape[:3] + (groups, block))
    mine = lax.dynamic_slice_in_dim(rest, lax.axis_index("y") * part, part, 4)
    return both[..., :LAT], mine


def partial_attention(queries, cache, lengths, positions):
    steps, seqs, heads_dev, _ = queries.shape
    ctx_dev = cache.shape[1]
    floats = queries.astype(jnp.float32)
    decode_step_position = (
        positions[None, :] + jnp.arange(steps, dtype=jnp.int32)[:, None]
    ).astype(jnp.float32)[:, :, None]
    rotated = jnp.concatenate(
        [floats[..., :LAT], rotate(floats[..., LAT:], decode_step_position)], axis=-1
    ).astype(jnp.bfloat16)
    rows = jnp.transpose(rotated, (1, 0, 2, 3)).reshape(seqs, steps * heads_dev, LAT + ROPE)
    scores = (
        jnp.einsum("eic,ezc->eiz", rows, cache, preferred_element_type=jnp.float32) * score_scale
    )
    scores = scores.reshape(seqs, steps, heads_dev, ctx_dev)
    places = lax.axis_index(CONTEXT) * ctx_dev + jnp.arange(ctx_dev, dtype=jnp.int32)
    limit = lengths[:, None] - 1 + jnp.arange(steps, dtype=jnp.int32)[None, :]
    valid = places[None, None, None, :] < limit[:, :, None, None]
    masked = jnp.where(valid, scores, neg_large)
    top = jnp.max(masked, axis=-1)
    weight = jnp.where(valid, jnp.exp(masked - top[..., None]), 0.0)
    total = jnp.sum(weight, axis=-1)
    weight_rows = weight.astype(jnp.bfloat16).reshape(seqs, steps * heads_dev, ctx_dev)
    sums = jnp.einsum(
        "bqj,bjl->bql", weight_rows, cache[:, :, :LAT], preferred_element_type=jnp.float32
    ).reshape(seqs, steps, heads_dev, LAT)
    live = total > 0.0
    total = jnp.where(live, total, 1.0)
    level = jnp.where(live, top + jnp.log(total), neg_large)
    return sums / total[..., None], level


def in_parts(level):
    high = lax.reduce_precision(level, 8, 7)
    rest = level - high
    middle = lax.reduce_precision(rest, 8, 7)
    return high, middle, rest - middle


def local(queries, cache, lengths, positions, up_weight, out_weight):
    steps, seqs, heads_dev, _ = queries.shape
    width = out_weight.shape[2]
    groups = lax.axis_size("x") * lax.axis_size("c")
    up, out = of_columns(up_weight, out_weight, groups)

    latents, level = partial_attention(queries, cache, lengths, positions)
    parts = jnp.stack(in_parts(level), axis=-1)
    parts = jnp.pad(parts, ((0, 0), (0, 0), (0, 0), (0, LANES - 3)))
    packet = jnp.concatenate([latents, parts], axis=-1).astype(jnp.bfloat16)
    rows = steps * seqs // NY
    packet = packet.reshape(seqs // rows, rows, steps, heads_dev, LAT + LANES)
    packet = jnp.transpose(packet, (2, 0, 3, 1, 4)).reshape(NY * NZ, rows, LAT + LANES)
    came = exchange(packet, CONTEXT).astype(jnp.float32)
    levels = came[..., LAT] + came[..., LAT + 1] + came[..., LAT + 2]
    share = jnp.exp(levels - jnp.max(levels, axis=0, keepdims=True))
    share = share / jnp.sum(share, axis=0, keepdims=True)
    latent = jnp.sum(came[..., :LAT] * share[..., None], axis=0).astype(jnp.bfloat16)
    latent, up, out = lax.optimization_barrier((gather(latent, CONTEXT, NY * NZ), up, out))
    latent = latent.reshape(NY, NZ, rows, LAT)

    values = jnp.einsum(
        "yhrl,shvl->yrshv", latent, up, preferred_element_type=jnp.float32
    ).astype(jnp.bfloat16)
    partial = jnp.einsum(
        "yrshv,shvgd->gyrd", values, out, preferred_element_type=jnp.float32
    ).astype(jnp.bfloat16)
    partial = partial.reshape(groups, NY * rows, -1)
    mine = jnp.sum(exchange(partial, HEAD).astype(jnp.float32), axis=0).astype(jnp.bfloat16)
    mine = jnp.sum(gather(mine, "z", NZ).astype(jnp.float32), axis=0).astype(jnp.bfloat16)
    whole = jnp.transpose(gather(mine, "y", NY).reshape(NY, NY * rows, -1), (1, 0, 2))
    return whole.reshape(steps, seqs, width // groups)


def solution(mesh):
    split = Mesh(mesh.devices.reshape(NY, NZ, -1, 2), ("y", "z", "x", "c"))
    return jax.shard_map(
        local,
        mesh=split,
        in_specs=(
            P(None, None, HEAD, None),
            P(None, CONTEXT, None),
            P(),
            P(),
            P(HEAD, CONTEXT, None),
            P(HEAD, CONTEXT, None),
        ),
        out_specs=P(None, None, HEAD),
        check_vma=False,
    )
```

```python
import math

import jax
import jax.numpy as jnp
from jax import lax
from jax.sharding import Mesh
from jax.sharding import PartitionSpec as P

LAT = 512
ROPE = 64
NY = 4
NB = 4
NL = 4
NZ = NB * NL
PIECES = 1
LANES = 128

CONTEXT = ("y", "b", "l")
ROW = ("b", "l")
FAR = ("y", "b")
HEAD = ("x", "c")

score_scale = 192.0 ** (-0.5)
neg_large = -1e30


def rotate(values, angle_pos):
    half = values.shape[-1] // 2
    freqs = jnp.exp(
        -jnp.arange(half, dtype=jnp.float32) * (2.0 / values.shape[-1]) * math.log(10000.0)
    )
    angles = angle_pos[..., None] * freqs
    cosine = jnp.cos(angles)
    sine = jnp.sin(angles)
    first = values[..., :half]
    second = values[..., half:]
    return jnp.concatenate(
        [first * cosine - second * sine, first * sine + second * cosine], axis=-1
    )


def exchange(array, axes):
    return lax.all_to_all(array, axes, 0, 0, tiled=True)


def gather(array, axis, size):
    return exchange(jnp.broadcast_to(array[None], (size,) + array.shape), axis)


def swap(blocks, axis, pieces):
    size = blocks.shape[0]
    me = lax.axis_index(axis)
    held = []
    for k in range(size):
        block = lax.dynamic_index_in_dim(blocks, me ^ k, 0, keepdims=False)
        parts = jnp.split(block, pieces, axis=0)
        if k:
            parts = [lax.ppermute(part, axis, [(i, i ^ k) for i in range(size)]) for part in parts]
        held.extend(parts)
    return held


def of_neighbours(up_weight, out_weight, groups):
    heads, count, width = out_weight.shape
    cut = out_weight.reshape(NB, NL, count, groups, NY, -1)
    cut = jnp.transpose(cut, (1, 4, 0, 2, 3, 5)).reshape(NL, NY, NB * count, -1)
    up = jnp.swapaxes(up_weight.reshape(NB, NL, count, LAT), 0, 1).reshape(NL, 1, NB * count, LAT)
    up = jnp.broadcast_to(up, (NL, NY, NB * count, LAT))
    return jnp.stack(swap(jnp.concatenate([up, cut], axis=-1), "l", 1), axis=1)


def partial_attention(queries, cache, lengths, positions):
    steps, seqs, heads_dev, _ = queries.shape
    ctx_dev = cache.shape[1]
    floats = queries.astype(jnp.float32)
    decode_step_position = (
        positions[None, :] + jnp.arange(steps, dtype=jnp.int32)[:, None]
    ).astype(jnp.float32)[:, :, None]
    rotated = jnp.concatenate(
        [floats[..., :LAT], rotate(floats[..., LAT:], decode_step_position)], axis=-1
    ).astype(jnp.bfloat16)
    rows = jnp.transpose(rotated, (1, 0, 2, 3)).reshape(seqs, steps * heads_dev, LAT + ROPE)
    scores = (
        jnp.einsum("eic,ezc->eiz", rows, cache, preferred_element_type=jnp.float32) * score_scale
    )
    scores = scores.reshape(seqs, steps, heads_dev, ctx_dev)
    places = lax.axis_index(CONTEXT) * ctx_dev + jnp.arange(ctx_dev, dtype=jnp.int32)
    limit = lengths[:, None] - 1 + jnp.arange(steps, dtype=jnp.int32)[None, :]
    valid = places[None, None, None, :] < limit[:, :, None, None]
    masked = jnp.where(valid, scores, neg_large)
    top = jnp.max(masked, axis=-1)
    weight = jnp.where(valid, jnp.exp(masked - top[..., None]), 0.0)
    total = jnp.sum(weight, axis=-1)
    weight_rows = weight.astype(jnp.bfloat16).reshape(seqs, steps * heads_dev, ctx_dev)
    sums = jnp.einsum(
        "bqj,bjl->bql", weight_rows, cache[:, :, :LAT], preferred_element_type=jnp.float32
    ).reshape(seqs, steps, heads_dev, LAT)
    live = total > 0.0
    total = jnp.where(live, total, 1.0)
    level = jnp.where(live, top + jnp.log(total), neg_large)
    return sums / total[..., None], level


def in_parts(level):
    high = lax.reduce_precision(level, 8, 7)
    rest = level - high
    middle = lax.reduce_precision(rest, 8, 7)
    return high, middle, rest - middle


def local(queries, cache, lengths, positions, up_weight, out_weight):
    steps, seqs, heads_dev, _ = queries.shape
    width = out_weight.shape[2]
    groups = lax.axis_size("x") * lax.axis_size("c")
    weights = of_neighbours(up_weight, out_weight, groups)

    latents, level = partial_attention(queries, cache, lengths, positions)
    parts = jnp.stack(in_parts(level), axis=-1)
    parts = jnp.pad(parts, ((0, 0), (0, 0), (0, 0), (0, LANES - 3)))
    packet = jnp.concatenate([latents, parts], axis=-1).astype(jnp.bfloat16)
    rows = steps * seqs // NY
    packet = packet.reshape(seqs // rows, rows, steps, heads_dev, LAT + LANES)
    packet = jnp.transpose(packet, (2, 0, 3, 1, 4)).reshape(NY * NZ, rows, LAT + LANES)
    came, weights = lax.optimization_barrier((exchange(packet, CONTEXT), weights))
    came = came.astype(jnp.float32)
    levels = came[..., LAT] + came[..., LAT + 1] + came[..., LAT + 2]
    share = jnp.exp(levels - jnp.max(levels, axis=0, keepdims=True))
    share = share / jnp.sum(share, axis=0, keepdims=True)
    latent = jnp.sum(came[..., :LAT] * share[..., None], axis=0).astype(jnp.bfloat16)
    copies = jnp.broadcast_to(latent[None], (NY * NB,) + latent.shape)
    copies, weights = lax.optimization_barrier((copies, weights))
    latent, weights = lax.optimization_barrier(
        (exchange(copies, FAR), swap(weights, "y", PIECES))
    )
    weights = jnp.concatenate([part.reshape(-1, part.shape[-1]) for part in weights], axis=0)
    up, out = weights[:, :LAT], weights[:, LAT:]
    latent = latent.reshape(NY, NB, rows, LAT)

    every = jnp.einsum("ybrl,kl->ybrk", latent, up, preferred_element_type=jnp.float32)
    place = (jnp.arange(up.shape[0], dtype=jnp.int32) // up_weight.shape[1]) % NB
    own = place[None, :] == jnp.arange(NB, dtype=jnp.int32)[:, None]
    values = jnp.sum(jnp.where(own[None, :, None, :], every, 0.0), axis=1).astype(jnp.bfloat16)
    partial = jnp.einsum(
        "yrk,kd->yrd", values, out, preferred_element_type=jnp.float32
    ).astype(jnp.bfloat16)
    partial = jnp.transpose(partial.reshape(NY * rows, groups, -1), (1, 0, 2))
    mine = jnp.sum(exchange(partial, HEAD).astype(jnp.float32), axis=0).astype(jnp.bfloat16)
    mine = jnp.sum(gather(mine, ROW, NZ).astype(jnp.float32), axis=0).astype(jnp.bfloat16)
    whole = jnp.transpose(gather(mine, "y", NY).reshape(NY, NY * rows, -1), (1, 0, 2))
    return whole.reshape(steps, seqs, width // groups)


def solution(mesh):
    split = Mesh(mesh.devices.reshape(NY, NB, NL, -1, 2), ("y", "b", "l", "x", "c"))
    return jax.shard_map(
        local,
        mesh=split,
        in_specs=(
            P(None, None, HEAD, None),
            P(None, CONTEXT, None),
            P(),
            P(),
            P(HEAD, CONTEXT, None),
            P(HEAD, CONTEXT, None),
        ),
        out_specs=P(None, None, HEAD),
        check_vma=False,
    )
```

```python
import math

import jax
import jax.numpy as jnp
from jax import lax
from jax.sharding import Mesh
from jax.sharding import PartitionSpec as P

LAT = 512
ROPE = 64
NY = 4
NZ = 16
LANES = 128

CONTEXT = ("y", "z")
HEAD = ("x", "c")

score_scale = 192.0 ** (-0.5)
neg_large = -1e30


def rotate(values, angle_pos):
    half = values.shape[-1] // 2
    freqs = jnp.exp(
        -jnp.arange(half, dtype=jnp.float32) * (2.0 / values.shape[-1]) * math.log(10000.0)
    )
    angles = angle_pos[..., None] * freqs
    cosine = jnp.cos(angles)
    sine = jnp.sin(angles)
    first = values[..., :half]
    second = values[..., half:]
    return jnp.concatenate(
        [first * cosine - second * sine, first * sine + second * cosine], axis=-1
    )


def exchange(array, axes):
    return lax.all_to_all(array, axes, 0, 0, tiled=True)


def gather(array, axis, size):
    return exchange(jnp.broadcast_to(array[None], (size,) + array.shape), axis)


def swap(blocks, axis):
    size = blocks.shape[0]
    me = lax.axis_index(axis)
    held = []
    for k in range(size):
        block = lax.dynamic_index_in_dim(blocks, me ^ k, 0, keepdims=False)
        if k:
            block = lax.ppermute(block, axis, [(i, i ^ k) for i in range(size)])
        held.append(block)
    return held


def by_columns(up_weight, out_weight, groups):
    heads, count, _ = out_weight.shape
    cut = jnp.transpose(out_weight.reshape(heads, count, groups, NY, -1), (3, 0, 1, 2, 4))
    cut = cut.reshape(NY, heads * count, -1)
    up = jnp.broadcast_to(up_weight.reshape(1, heads * count, LAT), (NY, heads * count, LAT))
    return jnp.concatenate([up, cut], axis=-1)


def partial_attention(queries, cache, lengths, positions):
    steps, seqs, heads_dev, _ = queries.shape
    ctx_dev = cache.shape[1]
    floats = queries.astype(jnp.float32)
    decode_step_position = (
        positions[None, :] + jnp.arange(steps, dtype=jnp.int32)[:, None]
    ).astype(jnp.float32)[:, :, None]
    rotated = jnp.concatenate(
        [floats[..., :LAT], rotate(floats[..., LAT:], decode_step_position)], axis=-1
    ).astype(jnp.bfloat16)
    rows = jnp.transpose(rotated, (1, 0, 2, 3)).reshape(seqs, steps * heads_dev, LAT + ROPE)
    scores = (
        jnp.einsum("eic,ezc->eiz", rows, cache, preferred_element_type=jnp.float32) * score_scale
    )
    scores = scores.reshape(seqs, steps, heads_dev, ctx_dev)
    places = lax.axis_index(CONTEXT) * ctx_dev + jnp.arange(ctx_dev, dtype=jnp.int32)
    limit = lengths[:, None] - 1 + jnp.arange(steps, dtype=jnp.int32)[None, :]
    valid = places[None, None, None, :] < limit[:, :, None, None]
    masked = jnp.where(valid, scores, neg_large)
    top = jnp.max(masked, axis=-1)
    weight = jnp.where(valid, jnp.exp(masked - top[..., None]), 0.0)
    total = jnp.sum(weight, axis=-1)
    weight_rows = weight.astype(jnp.bfloat16).reshape(seqs, steps * heads_dev, ctx_dev)
    sums = jnp.einsum(
        "bqj,bjl->bql", weight_rows, cache[:, :, :LAT], preferred_element_type=jnp.float32
    ).reshape(seqs, steps, heads_dev, LAT)
    live = total > 0.0
    total = jnp.where(live, total, 1.0)
    level = jnp.where(live, top + jnp.log(total), neg_large)
    return sums / total[..., None], level


def in_parts(level):
    high = lax.reduce_precision(level, 8, 7)
    rest = level - high
    middle = lax.reduce_precision(rest, 8, 7)
    return high, middle, rest - middle


def local(queries, cache, lengths, positions, up_weight, out_weight):
    steps, seqs, heads_dev, _ = queries.shape
    width = out_weight.shape[2]
    groups = lax.axis_size("x") * lax.axis_size("c")
    latents, level = partial_attention(queries, cache, lengths, positions)
    parts = jnp.stack(in_parts(level), axis=-1)
    parts = jnp.pad(parts, ((0, 0), (0, 0), (0, 0), (0, LANES - 3)))
    packet = jnp.concatenate([latents, parts], axis=-1).astype(jnp.bfloat16)
    rows = steps * seqs // NY
    packet = packet.reshape(seqs // rows, rows, steps, heads_dev, LAT + LANES)
    packet = jnp.transpose(packet, (2, 0, 3, 1, 4)).reshape(NY * NZ, rows, LAT + LANES)
    weights = swap(by_columns(up_weight, out_weight, groups), "y")
    came, weights = lax.optimization_barrier((exchange(packet, CONTEXT), weights))
    came = came.astype(jnp.float32)
    levels = came[..., LAT] + came[..., LAT + 1] + came[..., LAT + 2]
    share = jnp.exp(levels - jnp.max(levels, axis=0, keepdims=True))
    share = share / jnp.sum(share, axis=0, keepdims=True)
    latent = jnp.sum(came[..., :LAT] * share[..., None], axis=0).astype(jnp.bfloat16)
    weights = jnp.concatenate(weights, axis=0)
    latent, up, out = lax.optimization_barrier(
        (gather(latent, CONTEXT, NY * NZ), weights[:, :LAT], weights[:, LAT:])
    )
    latent = latent.reshape(NY, NZ, rows, LAT)

    every = jnp.einsum("yzrl,kl->yzrk", latent, up, preferred_element_type=jnp.float32)
    place = (jnp.arange(up.shape[0], dtype=jnp.int32) // up_weight.shape[1]) % NZ
    own = place[None, :] == jnp.arange(NZ, dtype=jnp.int32)[:, None]
    values = jnp.sum(jnp.where(own[None, :, None, :], every, 0.0), axis=1).astype(jnp.bfloat16)
    partial = jnp.einsum(
        "yrk,kd->yrd", values, out, preferred_element_type=jnp.float32
    ).astype(jnp.bfloat16)
    partial = jnp.transpose(partial.reshape(NY * rows, groups, -1), (1, 0, 2))
    mine = jnp.sum(exchange(partial, HEAD).astype(jnp.float32), axis=0).astype(jnp.bfloat16)
    mine = jnp.sum(gather(mine, "z", NZ).astype(jnp.float32), axis=0).astype(jnp.bfloat16)
    whole = jnp.transpose(gather(mine, "y", NY).reshape(NY, NY * rows, -1), (1, 0, 2))
    return whole.reshape(steps, seqs, width // groups)


def solution(mesh):
    split = Mesh(mesh.devices.reshape(NY, NZ, -1, 2), ("y", "z", "x", "c"))
    return jax.shard_map(
        local,
        mesh=split,
        in_specs=(
            P(None, None, HEAD, None),
            P(None, CONTEXT, None),
            P(),
            P(),
            P(HEAD, CONTEXT, None),
            P(HEAD, CONTEXT, None),
        ),
        out_specs=P(None, None, HEAD),
        check_vma=False,
    )
```

```python
import math

import jax
import jax.numpy as jnp
from jax import lax
from jax.sharding import Mesh
from jax.sharding import PartitionSpec as P

LAT = 512
ROPE = 64
NY = 4
NZ = 16
LANES = 128

CONTEXT = ("y", "z")
HEAD = ("x", "c")
PLANE = ("y", "x", "c")

score_scale = 192.0 ** (-0.5)
neg_large = -1e30


def rotate(values, angle_pos):
    half = values.shape[-1] // 2
    freqs = jnp.exp(
        -jnp.arange(half, dtype=jnp.float32) * (2.0 / values.shape[-1]) * math.log(10000.0)
    )
    angles = angle_pos[..., None] * freqs
    cosine = jnp.cos(angles)
    sine = jnp.sin(angles)
    first = values[..., :half]
    second = values[..., half:]
    return jnp.concatenate(
        [first * cosine - second * sine, first * sine + second * cosine], axis=-1
    )


def exchange(array, axes):
    return lax.all_to_all(array, axes, 0, 0, tiled=True)


def gather(array, axis, size):
    return exchange(jnp.broadcast_to(array[None], (size,) + array.shape), axis)


def swap(blocks, axis):
    size = blocks.shape[0]
    me = lax.axis_index(axis)
    held = []
    for k in range(size):
        block = lax.dynamic_index_in_dim(blocks, me ^ k, 0, keepdims=False)
        if k:
            block = lax.ppermute(block, axis, [(i, i ^ k) for i in range(size)])
        held.append(block)
    return held


def partial_attention(queries, cache, lengths, positions):
    steps, seqs, heads_dev, _ = queries.shape
    ctx_dev = cache.shape[1]
    floats = queries.astype(jnp.float32)
    decode_step_position = (
        positions[None, :] + jnp.arange(steps, dtype=jnp.int32)[:, None]
    ).astype(jnp.float32)[:, :, None]
    rotated = jnp.concatenate(
        [floats[..., :LAT], rotate(floats[..., LAT:], decode_step_position)], axis=-1
    ).astype(jnp.bfloat16)
    rows = jnp.transpose(rotated, (1, 0, 2, 3)).reshape(seqs, steps * heads_dev, LAT + ROPE)
    scores = (
        jnp.einsum("eic,ezc->eiz", rows, cache, preferred_element_type=jnp.float32) * score_scale
    )
    scores = scores.reshape(seqs, steps, heads_dev, ctx_dev)
    places = lax.axis_index(CONTEXT) * ctx_dev + jnp.arange(ctx_dev, dtype=jnp.int32)
    limit = lengths[:, None] - 1 + jnp.arange(steps, dtype=jnp.int32)[None, :]
    valid = places[None, None, None, :] < limit[:, :, None, None]
    masked = jnp.where(valid, scores, neg_large)
    top = jnp.max(masked, axis=-1)
    weight = jnp.where(valid, jnp.exp(masked - top[..., None]), 0.0)
    total = jnp.sum(weight, axis=-1)
    weight_rows = weight.astype(jnp.bfloat16).reshape(seqs, steps * heads_dev, ctx_dev)
    sums = jnp.einsum(
        "bqj,bjl->bql", weight_rows, cache[:, :, :LAT], preferred_element_type=jnp.float32
    ).reshape(seqs, steps, heads_dev, LAT)
    live = total > 0.0
    total = jnp.where(live, total, 1.0)
    level = jnp.where(live, top + jnp.log(total), neg_large)
    return sums / total[..., None], level


def in_parts(level):
    high = lax.reduce_precision(level, 8, 7)
    rest = level - high
    middle = lax.reduce_precision(rest, 8, 7)
    return high, middle, rest - middle


def local(queries, cache, lengths, positions, up_weight, out_weight):
    steps, seqs, heads_dev, _ = queries.shape
    width = out_weight.shape[2]
    groups = lax.axis_size("x") * lax.axis_size("c")
    latents, level = partial_attention(queries, cache, lengths, positions)
    parts = jnp.stack(in_parts(level), axis=-1)
    parts = jnp.pad(parts, ((0, 0), (0, 0), (0, 0), (0, LANES - 3)))
    packet = jnp.concatenate([latents, parts], axis=-1).astype(jnp.bfloat16)
    share_heads = heads_dev // NY
    packet = packet.reshape(seqs, steps, NY, share_heads, LAT + LANES)
    packet = jnp.transpose(packet, (2, 1, 0, 3, 4)).reshape(NY * NZ, share_heads, LAT + LANES)
    weights = jnp.concatenate([up_weight, out_weight], axis=-1).reshape(NY, -1, LAT + width)
    weights = swap(weights, "y")
    came, weights = lax.optimization_barrier((exchange(packet, CONTEXT), weights))
    came = came.astype(jnp.float32)
    levels = came[..., LAT] + came[..., LAT + 1] + came[..., LAT + 2]
    share = jnp.exp(levels - jnp.max(levels, axis=0, keepdims=True))
    share = share / jnp.sum(share, axis=0, keepdims=True)
    latent = jnp.sum(came[..., :LAT] * share[..., None], axis=0).astype(jnp.bfloat16)
    weights = jnp.concatenate(weights, axis=0)
    latent, weights = lax.optimization_barrier((gather(latent, "z", NZ), weights))
    up, out = weights[:, :LAT], weights[:, LAT:]

    every = jnp.einsum("bhl,kl->bhk", latent, up, preferred_element_type=jnp.float32)
    place = (jnp.arange(up.shape[0], dtype=jnp.int32) // up_weight.shape[1]) % share_heads
    own = place[None, :] == jnp.arange(share_heads, dtype=jnp.int32)[:, None]
    values = jnp.sum(jnp.where(own[None], every, 0.0), axis=1).astype(jnp.bfloat16)
    partial = jnp.dot(values, out, preferred_element_type=jnp.float32).astype(jnp.bfloat16)
    rows = steps * seqs // NY
    partial = partial.reshape(NY, rows, groups, width // groups)
    partial = jnp.transpose(partial, (0, 2, 1, 3)).reshape(NY * groups, rows, width // groups)
    mine = jnp.sum(exchange(partial, PLANE).astype(jnp.float32), axis=0).astype(jnp.bfloat16)
    mine = jnp.sum(gather(mine, "z", NZ).astype(jnp.float32), axis=0).astype(jnp.bfloat16)
    return gather(mine, "y", NY).reshape(steps, seqs, width // groups)


def solution(mesh):
    split = Mesh(mesh.devices.reshape(NY, NZ, -1, 2), ("y", "z", "x", "c"))
    return jax.shard_map(
        local,
        mesh=split,
        in_specs=(
            P(None, None, HEAD, None),
            P(None, CONTEXT, None),
            P(),
            P(),
            P(HEAD, CONTEXT, None),
            P(HEAD, CONTEXT, None),
        ),
        out_specs=P(None, None, HEAD),
        check_vma=False,
    )
```

```python
import math

import jax
import jax.numpy as jnp
from jax import lax
from jax.experimental import pallas as pl
from jax.experimental.pallas import tpu as pltpu
from jax.sharding import Mesh
from jax.sharding import PartitionSpec as P

LAT = 512
ROPE = 64
NY = 4
NZ = 16
LANES = 128

CONTEXT = ("y", "z")
HEAD = ("x", "c")
PLANE = ("y", "x", "c")

score_scale = 192.0 ** (-0.5)
neg_large = -1e30


def turns(positions, steps):
    freqs = jnp.exp(
        -jnp.arange(ROPE // 2, dtype=jnp.float32) * (2.0 / ROPE) * math.log(10000.0)
    )
    at = (positions[None, :] + jnp.arange(steps, dtype=jnp.int32)[:, None]).astype(jnp.float32)
    angles = at[:, :, None] * freqs
    cosine = jnp.cos(angles)
    sine = jnp.sin(angles)
    return jnp.concatenate([cosine, cosine], -1), jnp.concatenate([-sine, sine], -1)


def exchange(array, axes):
    return lax.all_to_all(array, axes, 0, 0, tiled=True)


def gather(array, axis, size):
    return exchange(jnp.broadcast_to(array[None], (size,) + array.shape), axis)


def swap(blocks, axis):
    size = blocks.shape[0]
    me = lax.axis_index(axis)
    held = []
    for k in range(size):
        block = lax.dynamic_index_in_dim(blocks, me ^ k, 0, keepdims=False)
        if k:
            block = lax.ppermute(block, axis, [(i, i ^ k) for i in range(size)])
        held.append(block)
    return held


def attend(queries_ref, keys_ref, cosine_ref, sine_ref, lengths_ref, out_ref):
    steps, seqs, heads, _ = queries_ref.shape
    ctx = keys_ref.shape[2]
    here = lax.axis_index(CONTEXT) * ctx
    place = here + lax.broadcasted_iota(jnp.int32, (heads, ctx), 1)
    near = lax.broadcasted_iota(jnp.int32, (ROPE, ROPE), 0)
    far = lax.broadcasted_iota(jnp.int32, (ROPE, ROPE), 1)
    turn = ((near + ROPE // 2) % ROPE == far).astype(jnp.float32).astype(jnp.bfloat16)
    lane = lax.broadcasted_iota(jnp.int32, (steps * heads, LANES), 1)
    for b in range(seqs):
        plain = [queries_ref[s, b, :, :LAT] for s in range(steps)]
        turned = []
        for s in range(steps):
            tail = queries_ref[s, b, :, LAT:]
            other = jnp.dot(tail, turn, preferred_element_type=jnp.float32)
            cosine = cosine_ref[s, b : b + 1, :]
            sine = sine_ref[s, b : b + 1, :]
            turned.append((tail.astype(jnp.float32) * cosine + other * sine).astype(jnp.bfloat16))
        keys = keys_ref[b]
        scores = jnp.dot(
            jnp.concatenate(plain, axis=0), keys[:LAT], preferred_element_type=jnp.float32
        ) + jnp.dot(jnp.concatenate(turned, axis=0), keys[LAT:], preferred_element_type=jnp.float32)
        scores = scores * score_scale
        valid = jnp.concatenate([place < lengths_ref[b] - 1 + s for s in range(steps)], axis=0)
        masked = jnp.where(valid, scores, neg_large)
        top = jnp.max(masked, axis=-1, keepdims=True)
        weight = jnp.where(valid, jnp.exp(masked - top), 0.0)
        total = jnp.sum(weight, axis=-1, keepdims=True)
        sums = lax.dot_general(
            weight.astype(jnp.bfloat16), keys[:LAT], (((1,), (1,)), ((), ())),
            preferred_element_type=jnp.float32,
        )
        live = total > 0.0
        total = jnp.where(live, total, 1.0)
        level = jnp.where(live, top + jnp.log(total), neg_large)
        high = level.astype(jnp.bfloat16).astype(jnp.float32)
        rest = level - high
        middle = rest.astype(jnp.bfloat16).astype(jnp.float32)
        low = rest - middle
        parts = jnp.where(lane == 0, high, jnp.where(lane == 1, middle, low)).astype(jnp.bfloat16)
        latents = (sums / total).astype(jnp.bfloat16)
        for s in range(steps):
            rows = slice(s * heads, (s + 1) * heads)
            out_ref[s * seqs + b, :, :LAT] = latents[rows]
            out_ref[s * seqs + b, :, LAT:] = parts[rows]


def combine(came_ref, out_ref):
    came = came_ref[:, :, LAT:].astype(jnp.float32)
    levels = came[:, :, 0:1] + came[:, :, 1:2] + came[:, :, 2:3]
    share = jnp.exp(levels - jnp.max(levels, axis=0, keepdims=True))
    share = share / jnp.sum(share, axis=0, keepdims=True)
    latent = jnp.sum(came_ref[:, :, :LAT].astype(jnp.float32) * share, axis=0)
    out_ref[...] = jnp.broadcast_to(latent.astype(jnp.bfloat16)[None], out_ref.shape)


def whole(memory):
    return pl.BlockSpec(memory_space=memory)


def local(queries, cache, lengths, positions, up_weight, out_weight):
    steps, seqs, heads_dev, _ = queries.shape
    width = out_weight.shape[2]
    groups = lax.axis_size("x") * lax.axis_size("c")
    cosine, sine = turns(positions, steps)
    packet = pl.pallas_call(
        attend,
        out_shape=jax.ShapeDtypeStruct((NZ, heads_dev, LAT + LANES), jnp.bfloat16),
        in_specs=[whole(pltpu.VMEM)] * 4 + [whole(pltpu.SMEM)],
        out_specs=whole(pltpu.VMEM),
        compiler_params=pltpu.CompilerParams(vmem_limit_bytes=32 * 1024 * 1024),
        cost_estimate=pl.CostEstimate(
            flops=140_000_000, bytes_accessed=3_000_000, transcendentals=70_000
        ),
    )(queries, jnp.swapaxes(cache, 1, 2), cosine, sine, lengths)
    share_heads = heads_dev // NY
    packet = packet.reshape(NZ, NY, share_heads, LAT + LANES)
    packet = jnp.swapaxes(packet, 0, 1).reshape(NY * NZ, share_heads, LAT + LANES)
    weights = jnp.concatenate([up_weight, out_weight], axis=-1).reshape(NY, -1, LAT + width)
    weights = swap(weights, "y")
    came, weights = lax.optimization_barrier((exchange(packet, CONTEXT), weights))
    copies = pl.pallas_call(
        combine,
        out_shape=jax.ShapeDtypeStruct((NZ, share_heads, LAT), jnp.bfloat16),
        in_specs=[whole(pltpu.VMEM)],
        out_specs=whole(pltpu.VMEM),
        compiler_params=pltpu.CompilerParams(vmem_limit_bytes=32 * 1024 * 1024),
        cost_estimate=pl.CostEstimate(
            flops=300_000, bytes_accessed=500_000, transcendentals=300
        ),
    )(came)
    weights = jnp.concatenate(weights, axis=0)
    latent, weights = lax.optimization_barrier((exchange(copies, "z"), weights))
    up, out = weights[:, :LAT], weights[:, LAT:]

    every = jnp.einsum("bhl,kl->bhk", latent, up, preferred_element_type=jnp.float32)
    place = (jnp.arange(up.shape[0], dtype=jnp.int32) // up_weight.shape[1]) % share_heads
    own = place[None, :] == jnp.arange(share_heads, dtype=jnp.int32)[:, None]
    values = jnp.sum(jnp.where(own[None], every, 0.0), axis=1).astype(jnp.bfloat16)
    partial = jnp.dot(values, out, preferred_element_type=jnp.float32).astype(jnp.bfloat16)
    rows = steps * seqs // NY
    partial = partial.reshape(NY, rows, groups, width // groups)
    partial = jnp.transpose(partial, (0, 2, 1, 3)).reshape(NY * groups, rows, width // groups)
    mine = jnp.sum(exchange(partial, PLANE).astype(jnp.float32), axis=0).astype(jnp.bfloat16)
    mine = jnp.sum(gather(mine, "z", NZ).astype(jnp.float32), axis=0).astype(jnp.bfloat16)
    return gather(mine, "y", NY).reshape(steps, seqs, width // groups)


def solution(mesh):
    split = Mesh(mesh.devices.reshape(NY, NZ, -1, 2), ("y", "z", "x", "c"))
    return jax.shard_map(
        local,
        mesh=split,
        in_specs=(
            P(None, None, HEAD, None),
            P(None, CONTEXT, None),
            P(),
            P(),
            P(HEAD, CONTEXT, None),
            P(HEAD, CONTEXT, None),
        ),
        out_specs=P(None, None, HEAD),
        check_vma=False,
    )
```

```python
import math

import jax
import jax.numpy as jnp
from jax import lax
from jax.experimental import pallas as pl
from jax.experimental.pallas import tpu as pltpu
from jax.sharding import Mesh
from jax.sharding import PartitionSpec as P

LAT = 512
ROPE = 64
NY = 4
NZ = 16
LANES = 128

CONTEXT = ("y", "z")
HEAD = ("x", "c")
PLANE = ("y", "x", "c")

score_scale = 192.0 ** (-0.5)
neg_large = -1e30


def exchange(array, axes):
    return lax.all_to_all(array, axes, 0, 0, tiled=True)


def gather(array, axis, size):
    return exchange(jnp.broadcast_to(array[None], (size,) + array.shape), axis)


def swap(blocks, axis):
    size = blocks.shape[0]
    me = lax.axis_index(axis)
    held = []
    for k in range(size):
        block = lax.dynamic_index_in_dim(blocks, me ^ k, 0, keepdims=False)
        if k:
            block = lax.ppermute(block, axis, [(i, i ^ k) for i in range(size)])
        held.append(block)
    return held


def turns(positions, steps, seqs):
    half = ROPE // 2
    shape = (steps * seqs, ROPE)
    row = lax.broadcasted_iota(jnp.int32, shape, 0)
    lane = lax.broadcasted_iota(jnp.int32, shape, 1)
    at = jnp.zeros(shape, jnp.int32)
    for b in range(seqs):
        for s in range(steps):
            at = jnp.where(row == s * seqs + b, positions[b] + s, at)
    freqs = jnp.zeros(shape, jnp.float32)
    for i in range(half):
        freqs = jnp.where(lane % half == i, 10000.0 ** (-2.0 * i / ROPE), freqs)
    angles = at.astype(jnp.float32) * freqs
    rounds = jnp.floor(angles * (0.5 / math.pi) + 0.5)
    high = 6.28125
    middle = 1981.0 / 2**20
    low = 2.0 * math.pi - high - middle
    angles = ((angles - rounds * high) - rounds * middle) - rounds * low
    sine = jnp.sin(angles)
    return jnp.cos(angles), jnp.where(lane < half, -sine, sine)


def attend(queries_hbm, keys_hbm, lengths_hbm, positions_hbm, out_ref,
           queries_ref, keys_ref, lengths_ref, positions_ref, sems):
    steps, seqs, heads, _ = queries_ref.shape
    ctx = keys_ref.shape[2]
    copies = [
        pltpu.make_async_copy(positions_hbm, positions_ref, sems.at[0]),
        pltpu.make_async_copy(lengths_hbm, lengths_ref, sems.at[1]),
        pltpu.make_async_copy(queries_hbm, queries_ref, sems.at[2]),
    ]
    for b in range(seqs):
        copies.append(pltpu.make_async_copy(keys_hbm.at[b], keys_ref.at[b], sems.at[3 + b]))
    for copy in copies:
        copy.start()
    copies[0].wait()
    cosines, sines = turns(positions_ref, steps, seqs)
    copies[1].wait()
    copies[2].wait()
    here = lax.axis_index(CONTEXT) * ctx
    place = here + lax.broadcasted_iota(jnp.int32, (heads, ctx), 1)
    near = lax.broadcasted_iota(jnp.int32, (ROPE, ROPE), 0)
    far = lax.broadcasted_iota(jnp.int32, (ROPE, ROPE), 1)
    turn = ((near + ROPE // 2) % ROPE == far).astype(jnp.float32).astype(jnp.bfloat16)
    lane = lax.broadcasted_iota(jnp.int32, (steps * heads, LANES), 1)
    for b in range(seqs):
        copies[3 + b].wait()
        plain = [queries_ref[s, b, :, :LAT] for s in range(steps)]
        turned = []
        for s in range(steps):
            tail = queries_ref[s, b, :, LAT:]
            other = jnp.dot(tail, turn, preferred_element_type=jnp.float32)
            cosine = cosines[s * seqs + b : s * seqs + b + 1]
            sine = sines[s * seqs + b : s * seqs + b + 1]
            turned.append((tail.astype(jnp.float32) * cosine + other * sine).astype(jnp.bfloat16))
        keys = keys_ref[b]
        scores = jnp.dot(
            jnp.concatenate(plain, axis=0), keys[:LAT], preferred_element_type=jnp.float32
        ) + jnp.dot(jnp.concatenate(turned, axis=0), keys[LAT:], preferred_element_type=jnp.float32)
        scores = scores * score_scale
        valid = jnp.concatenate([place < lengths_ref[b] - 1 + s for s in range(steps)], axis=0)
        masked = jnp.where(valid, scores, neg_large)
        top = jnp.max(masked, axis=-1, keepdims=True)
        weight = jnp.where(valid, jnp.exp(masked - top), 0.0)
        total = jnp.sum(weight, axis=-1, keepdims=True)
        sums = lax.dot_general(
            weight.astype(jnp.bfloat16), keys[:LAT], (((1,), (1,)), ((), ())),
            preferred_element_type=jnp.float32,
        )
        live = total > 0.0
        total = jnp.where(live, total, 1.0)
        level = jnp.where(live, top + jnp.log(total), neg_large)
        high = level.astype(jnp.bfloat16).astype(jnp.float32)
        rest = level - high
        middle = rest.astype(jnp.bfloat16).astype(jnp.float32)
        low = rest - middle
        parts = jnp.where(lane == 0, high, jnp.where(lane == 1, middle, low)).astype(jnp.bfloat16)
        latents = (sums / total).astype(jnp.bfloat16)
        for s in range(steps):
            for y in range(NY):
                rows = slice(s * heads + y * (heads // NY), s * heads + (y + 1) * (heads // NY))
                out_ref[y * steps * seqs + s * seqs + b, :, :LAT] = latents[rows]
                out_ref[y * steps * seqs + s * seqs + b, :, LAT:] = parts[rows]


def combine(came_ref, out_ref):
    came = came_ref[:, :, LAT:].astype(jnp.float32)
    levels = came[:, :, 0:1] + came[:, :, 1:2] + came[:, :, 2:3]
    share = jnp.exp(levels - jnp.max(levels, axis=0, keepdims=True))
    share = share / jnp.sum(share, axis=0, keepdims=True)
    latent = jnp.sum(came_ref[:, :, :LAT].astype(jnp.float32) * share, axis=0)
    out_ref[...] = jnp.broadcast_to(latent.astype(jnp.bfloat16)[None], out_ref.shape)


def whole(memory):
    return pl.BlockSpec(memory_space=memory)


def local(queries, cache, lengths, positions, up_weight, out_weight):
    steps, seqs, heads_dev, _ = queries.shape
    width = out_weight.shape[2]
    groups = lax.axis_size("x") * lax.axis_size("c")
    share_heads = heads_dev // NY
    keys = jnp.swapaxes(cache, 1, 2)
    packet = pl.pallas_call(
        attend,
        out_shape=jax.ShapeDtypeStruct((NY * NZ, share_heads, LAT + LANES), jnp.bfloat16),
        in_specs=[whole(pl.ANY)] * 4,
        out_specs=whole(pltpu.VMEM),
        scratch_shapes=[
            pltpu.VMEM(queries.shape, queries.dtype),
            pltpu.VMEM(keys.shape, keys.dtype),
            pltpu.SMEM(lengths.shape, lengths.dtype),
            pltpu.SMEM(positions.shape, positions.dtype),
            pltpu.SemaphoreType.DMA((3 + seqs,)),
        ],
        compiler_params=pltpu.CompilerParams(vmem_limit_bytes=60 * 1024 * 1024),
        cost_estimate=pl.CostEstimate(
            flops=140_000_000, bytes_accessed=3_000_000, transcendentals=70_000
        ),
    )(queries, keys, lengths, positions)
    weights = jnp.concatenate([up_weight, out_weight], axis=-1).reshape(NY, -1, LAT + width)
    weights = swap(weights, "y")
    came, weights = lax.optimization_barrier((exchange(packet, CONTEXT), weights))
    copies = pl.pallas_call(
        combine,
        out_shape=jax.ShapeDtypeStruct((NZ, share_heads, LAT), jnp.bfloat16),
        in_specs=[whole(pltpu.VMEM)],
        out_specs=whole(pltpu.VMEM),
        compiler_params=pltpu.CompilerParams(vmem_limit_bytes=32 * 1024 * 1024),
        cost_estimate=pl.CostEstimate(
            flops=300_000, bytes_accessed=500_000, transcendentals=300
        ),
    )(came)
    weights = jnp.concatenate(weights, axis=0)
    latent, weights = lax.optimization_barrier((exchange(copies, "z"), weights))
    up, out = weights[:, :LAT], weights[:, LAT:]

    every = jnp.einsum("bhl,kl->bhk", latent, up, preferred_element_type=jnp.float32)
    place = (jnp.arange(up.shape[0], dtype=jnp.int32) // up_weight.shape[1]) % share_heads
    own = place[None, :] == jnp.arange(share_heads, dtype=jnp.int32)[:, None]
    values = jnp.sum(jnp.where(own[None], every, 0.0), axis=1).astype(jnp.bfloat16)
    partial = jnp.dot(values, out, preferred_element_type=jnp.float32).astype(jnp.bfloat16)
    rows = steps * seqs // NY
    partial = partial.reshape(NY, rows, groups, width // groups)
    partial = jnp.transpose(partial, (0, 2, 1, 3)).reshape(NY * groups, rows, width // groups)
    mine = jnp.sum(exchange(partial, PLANE).astype(jnp.float32), axis=0).astype(jnp.bfloat16)
    mine = jnp.sum(gather(mine, "z", NZ).astype(jnp.float32), axis=0).astype(jnp.bfloat16)
    return gather(mine, "y", NY).reshape(steps, seqs, width // groups)


def solution(mesh):
    split = Mesh(mesh.devices.reshape(NY, NZ, -1, 2), ("y", "z", "x", "c"))
    return jax.shard_map(
        local,
        mesh=split,
        in_specs=(
            P(None, None, HEAD, None),
            P(None, CONTEXT, None),
            P(),
            P(),
            P(HEAD, CONTEXT, None),
            P(HEAD, CONTEXT, None),
        ),
        out_specs=P(None, None, HEAD),
        check_vma=False,
    )
```

```python
import math

import jax
import jax.numpy as jnp
from jax import lax
from jax.experimental import pallas as pl
from jax.experimental.pallas import tpu as pltpu
from jax.sharding import Mesh
from jax.sharding import PartitionSpec as P

LAT = 512
ROPE = 64
NY = 4
NZ = 16
LANES = 128

CONTEXT = ("y", "z")
HEAD = ("x", "c")
PLANE = ("y", "x", "c")

score_scale = 192.0 ** (-0.5)
neg_large = -1e30


def exchange(array, axes):
    return lax.all_to_all(array, axes, 0, 0, tiled=True)


def gather(array, axis, size):
    return exchange(jnp.broadcast_to(array[None], (size,) + array.shape), axis)


def swap(blocks, axis):
    size = blocks.shape[0]
    me = lax.axis_index(axis)
    held = []
    for k in range(size):
        block = lax.dynamic_index_in_dim(blocks, me ^ k, 0, keepdims=False)
        if k:
            block = lax.ppermute(block, axis, [(i, i ^ k) for i in range(size)])
        held.append(block)
    return held


def turns(positions, steps, seqs):
    half = ROPE // 2
    shape = (steps * seqs, ROPE)
    row = lax.broadcasted_iota(jnp.int32, shape, 0)
    lane = lax.broadcasted_iota(jnp.int32, shape, 1)
    at = jnp.zeros(shape, jnp.int32)
    for b in range(seqs):
        for s in range(steps):
            at = jnp.where(row == s * seqs + b, positions[b] + s, at)
    freqs = jnp.zeros(shape, jnp.float32)
    for i in range(half):
        freqs = jnp.where(lane % half == i, 10000.0 ** (-2.0 * i / ROPE), freqs)
    angles = at.astype(jnp.float32) * freqs
    rounds = jnp.floor(angles * (0.5 / math.pi) + 0.5)
    high = 6.28125
    middle = 1981.0 / 2**20
    low = 2.0 * math.pi - high - middle
    angles = ((angles - rounds * high) - rounds * middle) - rounds * low
    sine = jnp.sin(angles)
    return jnp.cos(angles), jnp.where(lane < half, -sine, sine)


def attend(queries_hbm, keys_hbm, lengths_hbm, positions_hbm, out_ref,
           queries_ref, keys_ref, lengths_ref, positions_ref, sems):
    steps, seqs, heads, _ = queries_ref.shape
    ctx = keys_ref.shape[2]
    copies = [
        pltpu.make_async_copy(positions_hbm, positions_ref, sems.at[0]),
        pltpu.make_async_copy(lengths_hbm, lengths_ref, sems.at[1]),
        pltpu.make_async_copy(queries_hbm, queries_ref, sems.at[2]),
    ]
    for b in range(seqs):
        copies.append(pltpu.make_async_copy(keys_hbm.at[b], keys_ref.at[b], sems.at[3 + b]))
    for copy in copies:
        copy.start()
    copies[0].wait()
    cosines, sines = turns(positions_ref, steps, seqs)
    for copy in copies[1:]:
        copy.wait()
    here = lax.axis_index(CONTEXT) * ctx
    place = here + lax.broadcasted_iota(jnp.int32, (heads, ctx), 1)
    near = lax.broadcasted_iota(jnp.int32, (ROPE, ROPE), 0)
    far = lax.broadcasted_iota(jnp.int32, (ROPE, ROPE), 1)
    turn = ((near + ROPE // 2) % ROPE == far).astype(jnp.float32).astype(jnp.bfloat16)
    lane = lax.broadcasted_iota(jnp.int32, (steps * heads, LANES), 1)
    tails = queries_ref[:, :, :, LAT:].reshape(steps * seqs * heads, ROPE)
    others = jnp.dot(tails, turn, preferred_element_type=jnp.float32)
    groups = (steps * seqs, heads, ROPE)
    turned = tails.astype(jnp.float32).reshape(groups) * cosines[:, None, :]
    turned = (turned + others.reshape(groups) * sines[:, None, :]).astype(jnp.bfloat16)
    scores = []
    for b in range(seqs):
        plain = jnp.concatenate([queries_ref[s, b, :, :LAT] for s in range(steps)], axis=0)
        tail = jnp.concatenate([turned[s * seqs + b] for s in range(steps)], axis=0)
        both = jnp.dot(plain, keys_ref[b, :LAT], preferred_element_type=jnp.float32)
        both += jnp.dot(tail, keys_ref[b, LAT:], preferred_element_type=jnp.float32)
        scores.append(both * score_scale)
    weights, totals, tops = [], [], []
    for b in range(seqs):
        valid = jnp.concatenate([place < lengths_ref[b] - 1 + s for s in range(steps)], axis=0)
        masked = jnp.where(valid, scores[b], neg_large)
        tops.append(jnp.max(masked, axis=-1, keepdims=True))
        weights.append(jnp.where(valid, jnp.exp(masked - tops[b]), 0.0))
        totals.append(jnp.sum(weights[b], axis=-1, keepdims=True))
    sums = [
        lax.dot_general(
            weights[b].astype(jnp.bfloat16), keys_ref[b, :LAT], (((1,), (1,)), ((), ())),
            preferred_element_type=jnp.float32,
        )
        for b in range(seqs)
    ]
    for b in range(seqs):
        live = totals[b] > 0.0
        total = jnp.where(live, totals[b], 1.0)
        level = jnp.where(live, tops[b] + jnp.log(total), neg_large)
        high = level.astype(jnp.bfloat16).astype(jnp.float32)
        rest = level - high
        middle = rest.astype(jnp.bfloat16).astype(jnp.float32)
        parts = jnp.where(lane == 0, high, jnp.where(lane == 1, middle, rest - middle))
        parts = parts.astype(jnp.bfloat16)
        latents = (sums[b] * (1.0 / total)).astype(jnp.bfloat16)
        for s in range(steps):
            for y in range(NY):
                rows = slice(s * heads + y * (heads // NY), s * heads + (y + 1) * (heads // NY))
                out_ref[y * steps * seqs + s * seqs + b, :, :LAT] = latents[rows]
                out_ref[y * steps * seqs + s * seqs + b, :, LAT:] = parts[rows]


def combine(came_ref, out_ref):
    came = came_ref[:, :, LAT:].astype(jnp.float32)
    levels = came[:, :, 0:1] + came[:, :, 1:2] + came[:, :, 2:3]
    share = jnp.exp(levels - jnp.max(levels, axis=0, keepdims=True))
    share = share / jnp.sum(share, axis=0, keepdims=True)
    latent = jnp.sum(came_ref[:, :, :LAT].astype(jnp.float32) * share, axis=0)
    out_ref[...] = jnp.broadcast_to(latent.astype(jnp.bfloat16)[None], out_ref.shape)


def whole(memory):
    return pl.BlockSpec(memory_space=memory)


def local(queries, cache, lengths, positions, up_weight, out_weight):
    steps, seqs, heads_dev, _ = queries.shape
    width = out_weight.shape[2]
    groups = lax.axis_size("x") * lax.axis_size("c")
    share_heads = heads_dev // NY
    keys = jnp.swapaxes(cache, 1, 2)
    packet = pl.pallas_call(
        attend,
        out_shape=jax.ShapeDtypeStruct((NY * NZ, share_heads, LAT + LANES), jnp.bfloat16),
        in_specs=[whole(pl.ANY)] * 4,
        out_specs=whole(pltpu.VMEM),
        scratch_shapes=[
            pltpu.VMEM(queries.shape, queries.dtype),
            pltpu.VMEM(keys.shape, keys.dtype),
            pltpu.SMEM(lengths.shape, lengths.dtype),
            pltpu.SMEM(positions.shape, positions.dtype),
            pltpu.SemaphoreType.DMA((3 + seqs,)),
        ],
        compiler_params=pltpu.CompilerParams(vmem_limit_bytes=60 * 1024 * 1024),
        cost_estimate=pl.CostEstimate(
            flops=140_000_000, bytes_accessed=3_000_000, transcendentals=70_000
        ),
    )(queries, keys, lengths, positions)
    weights = jnp.concatenate([up_weight, out_weight], axis=-1).reshape(NY, -1, LAT + width)
    weights = swap(weights, "y")
    came, weights = lax.optimization_barrier((exchange(packet, CONTEXT), weights))
    copies = pl.pallas_call(
        combine,
        out_shape=jax.ShapeDtypeStruct((NZ, share_heads, LAT), jnp.bfloat16),
        in_specs=[whole(pltpu.VMEM)],
        out_specs=whole(pltpu.VMEM),
        compiler_params=pltpu.CompilerParams(vmem_limit_bytes=32 * 1024 * 1024),
        cost_estimate=pl.CostEstimate(
            flops=300_000, bytes_accessed=500_000, transcendentals=300
        ),
    )(came)
    weights = jnp.concatenate(weights, axis=0)
    latent, weights = lax.optimization_barrier((exchange(copies, "z"), weights))
    up, out = weights[:, :LAT], weights[:, LAT:]

    every = jnp.einsum("bhl,kl->bhk", latent, up, preferred_element_type=jnp.float32)
    place = (jnp.arange(up.shape[0], dtype=jnp.int32) // up_weight.shape[1]) % share_heads
    own = place[None, :] == jnp.arange(share_heads, dtype=jnp.int32)[:, None]
    values = jnp.sum(jnp.where(own[None], every, 0.0), axis=1).astype(jnp.bfloat16)
    partial = jnp.dot(values, out, preferred_element_type=jnp.float32).astype(jnp.bfloat16)
    rows = steps * seqs // NY
    partial = partial.reshape(NY, rows, groups, width // groups)
    partial = jnp.transpose(partial, (0, 2, 1, 3)).reshape(NY * groups, rows, width // groups)
    mine = jnp.sum(exchange(partial, PLANE).astype(jnp.float32), axis=0).astype(jnp.bfloat16)
    mine = jnp.sum(gather(mine, "z", NZ).astype(jnp.float32), axis=0).astype(jnp.bfloat16)
    return gather(mine, "y", NY).reshape(steps, seqs, width // groups)


def solution(mesh):
    split = Mesh(mesh.devices.reshape(NY, NZ, -1, 2), ("y", "z", "x", "c"))
    return jax.shard_map(
        local,
        mesh=split,
        in_specs=(
            P(None, None, HEAD, None),
            P(None, CONTEXT, None),
            P(),
            P(),
            P(HEAD, CONTEXT, None),
            P(HEAD, CONTEXT, None),
        ),
        out_specs=P(None, None, HEAD),
        check_vma=False,
    )
```

```python
import math

import jax
import jax.numpy as jnp
from jax import lax
from jax.experimental import pallas as pl
from jax.experimental.pallas import tpu as pltpu
from jax.sharding import Mesh
from jax.sharding import PartitionSpec as P

LAT = 512
ROPE = 64
NY = 4
NZ = 16
LANES = 128

CONTEXT = ("y", "z")
HEAD = ("x", "c")
PLANE = ("y", "x", "c")

score_scale = 192.0 ** (-0.5)
neg_large = -1e30


def exchange(array, axes):
    return lax.all_to_all(array, axes, 0, 0, tiled=True)


def gather(array, axis, size):
    return exchange(jnp.broadcast_to(array[None], (size,) + array.shape), axis)


def swap(blocks, axis):
    size = blocks.shape[0]
    me = lax.axis_index(axis)
    held = []
    for k in range(size):
        block = lax.dynamic_index_in_dim(blocks, me ^ k, 0, keepdims=False)
        if k:
            block = lax.ppermute(block, axis, [(i, i ^ k) for i in range(size)])
        held.append(block)
    return held


def turns(positions, steps, seqs):
    half = ROPE // 2
    shape = (steps * seqs, ROPE)
    row = lax.broadcasted_iota(jnp.int32, shape, 0)
    lane = lax.broadcasted_iota(jnp.int32, shape, 1)
    at = jnp.zeros(shape, jnp.int32)
    for b in range(seqs):
        for s in range(steps):
            at = jnp.where(row == s * seqs + b, positions[b] + s, at)
    freqs = jnp.zeros(shape, jnp.float32)
    for i in range(half):
        freqs = jnp.where(lane % half == i, 10000.0 ** (-2.0 * i / ROPE), freqs)
    angles = at.astype(jnp.float32) * freqs
    rounds = jnp.floor(angles * (0.5 / math.pi) + 0.5)
    high = 6.28125
    middle = 1981.0 / 2**20
    low = 2.0 * math.pi - high - middle
    angles = ((angles - rounds * high) - rounds * middle) - rounds * low
    sine = jnp.sin(angles)
    return jnp.cos(angles), jnp.where(lane < half, -sine, sine)


def attend(queries_hbm, keys_hbm, lengths_hbm, positions_hbm, out_ref,
           queries_ref, keys_ref, lengths_ref, positions_ref, sems):
    steps, seqs, heads, _ = queries_ref.shape
    ctx = keys_ref.shape[2]
    copies = [
        pltpu.make_async_copy(positions_hbm, positions_ref, sems.at[0]),
        pltpu.make_async_copy(lengths_hbm, lengths_ref, sems.at[1]),
        pltpu.make_async_copy(queries_hbm, queries_ref, sems.at[2]),
    ]
    for b in range(seqs):
        copies.append(pltpu.make_async_copy(keys_hbm.at[b], keys_ref.at[b], sems.at[3 + b]))
    for copy in copies:
        copy.start()
    copies[0].wait()
    cosines, sines = turns(positions_ref, steps, seqs)
    for copy in copies[1:]:
        copy.wait()
    here = lax.axis_index(CONTEXT) * ctx
    place = here + lax.broadcasted_iota(jnp.int32, (heads, ctx), 1)
    near = lax.broadcasted_iota(jnp.int32, (ROPE, ROPE), 0)
    far = lax.broadcasted_iota(jnp.int32, (ROPE, ROPE), 1)
    turn = ((near + ROPE // 2) % ROPE == far).astype(jnp.float32).astype(jnp.bfloat16)
    lane = lax.broadcasted_iota(jnp.int32, (steps * heads, LANES), 1)
    tails = queries_ref[:, :, :, LAT:].reshape(steps * seqs * heads, ROPE)
    others = jnp.dot(tails, turn, preferred_element_type=jnp.float32)
    groups = (steps * seqs, heads, ROPE)
    turned = tails.astype(jnp.float32).reshape(groups) * cosines[:, None, :]
    turned = (turned + others.reshape(groups) * sines[:, None, :]).astype(jnp.bfloat16)
    scores = []
    for b in range(seqs):
        plain = jnp.concatenate([queries_ref[s, b, :, :LAT] for s in range(steps)], axis=0)
        tail = jnp.concatenate([turned[s * seqs + b] for s in range(steps)], axis=0)
        both = jnp.dot(plain, keys_ref[b, :LAT], preferred_element_type=jnp.float32)
        both += jnp.dot(tail, keys_ref[b, LAT:], preferred_element_type=jnp.float32)
        scores.append(both * score_scale)
    weights, totals, tops = [], [], []
    for b in range(seqs):
        valid = jnp.concatenate([place < lengths_ref[b] - 1 + s for s in range(steps)], axis=0)
        masked = jnp.where(valid, scores[b], neg_large)
        tops.append(jnp.max(masked, axis=-1, keepdims=True))
        weights.append(jnp.where(valid, jnp.exp(masked - tops[b]), 0.0))
        totals.append(jnp.sum(weights[b], axis=-1, keepdims=True))
    sums = [
        lax.dot_general(
            weights[b].astype(jnp.bfloat16), keys_ref[b, :LAT], (((1,), (1,)), ((), ())),
            preferred_element_type=jnp.float32,
        )
        for b in range(seqs)
    ]
    for b in range(seqs):
        live = totals[b] > 0.0
        total = jnp.where(live, totals[b], 1.0)
        level = jnp.where(live, tops[b] + jnp.log(total), neg_large)
        high = level.astype(jnp.bfloat16).astype(jnp.float32)
        rest = level - high
        middle = rest.astype(jnp.bfloat16).astype(jnp.float32)
        parts = jnp.where(lane == 0, high, jnp.where(lane == 1, middle, rest - middle))
        parts = parts.astype(jnp.bfloat16)
        latents = (sums[b] * (1.0 / total)).astype(jnp.bfloat16)
        for s in range(steps):
            for y in range(NY):
                rows = slice(s * heads + y * (heads // NY), s * heads + (y + 1) * (heads // NY))
                out_ref[y * steps * seqs + s * seqs + b, :, :LAT] = latents[rows]
                out_ref[y * steps * seqs + s * seqs + b, :, LAT:] = parts[rows]


def combine(came_ref, out_ref):
    came = came_ref[:, :, LAT:].astype(jnp.float32)
    levels = came[:, :, 0:1] + came[:, :, 1:2] + came[:, :, 2:3]
    share = jnp.exp(levels - jnp.max(levels, axis=0, keepdims=True))
    share = share / jnp.sum(share, axis=0, keepdims=True)
    latent = jnp.sum(came_ref[:, :, :LAT].astype(jnp.float32) * share, axis=0)
    out_ref[...] = jnp.broadcast_to(latent.astype(jnp.bfloat16)[None], out_ref.shape)


def whole(memory):
    return pl.BlockSpec(memory_space=memory)


def local(queries, cache, lengths, positions, up_weight, out_weight):
    steps, seqs, heads_dev, _ = queries.shape
    width = out_weight.shape[2]
    groups = lax.axis_size("x") * lax.axis_size("c")
    share_heads = heads_dev // NY
    keys = jnp.swapaxes(cache, 1, 2)
    packet = pl.pallas_call(
        attend,
        out_shape=jax.ShapeDtypeStruct((NY * NZ, share_heads, LAT + LANES), jnp.bfloat16),
        in_specs=[whole(pl.ANY)] * 4,
        out_specs=whole(pltpu.VMEM),
        scratch_shapes=[
            pltpu.VMEM(queries.shape, queries.dtype),
            pltpu.VMEM(keys.shape, keys.dtype),
            pltpu.SMEM(lengths.shape, lengths.dtype),
            pltpu.SMEM(positions.shape, positions.dtype),
            pltpu.SemaphoreType.DMA((3 + seqs,)),
        ],
        compiler_params=pltpu.CompilerParams(vmem_limit_bytes=60 * 1024 * 1024),
        cost_estimate=pl.CostEstimate(
            flops=140_000_000, bytes_accessed=3_000_000, transcendentals=70_000
        ),
    )(queries, keys, lengths, positions)
    weights = jnp.concatenate([up_weight, out_weight], axis=-1).reshape(NY, -1, LAT + width)
    weights = swap(weights, "y")
    came, early = lax.optimization_barrier((exchange(packet, CONTEXT), weights[:-2]))
    copies = pl.pallas_call(
        combine,
        out_shape=jax.ShapeDtypeStruct((NZ, share_heads, LAT), jnp.bfloat16),
        in_specs=[whole(pltpu.VMEM)],
        out_specs=whole(pltpu.VMEM),
        compiler_params=pltpu.CompilerParams(vmem_limit_bytes=32 * 1024 * 1024),
        cost_estimate=pl.CostEstimate(
            flops=300_000, bytes_accessed=500_000, transcendentals=300
        ),
    )(came)
    weights = jnp.concatenate(early + weights[-2:], axis=0)
    latent, weights = lax.optimization_barrier((exchange(copies, "z"), weights))
    up, out = weights[:, :LAT], weights[:, LAT:]

    every = jnp.einsum("bhl,kl->bhk", latent, up, preferred_element_type=jnp.float32)
    place = (jnp.arange(up.shape[0], dtype=jnp.int32) // up_weight.shape[1]) % share_heads
    own = place[None, :] == jnp.arange(share_heads, dtype=jnp.int32)[:, None]
    values = jnp.sum(jnp.where(own[None], every, 0.0), axis=1).astype(jnp.bfloat16)
    partial = jnp.dot(values, out, preferred_element_type=jnp.float32).astype(jnp.bfloat16)
    rows = steps * seqs // NY
    partial = partial.reshape(NY, rows, groups, width // groups)
    partial = jnp.transpose(partial, (0, 2, 1, 3)).reshape(NY * groups, rows, width // groups)
    mine = jnp.sum(exchange(partial, PLANE).astype(jnp.float32), axis=0).astype(jnp.bfloat16)
    mine = jnp.sum(gather(mine, "z", NZ).astype(jnp.float32), axis=0).astype(jnp.bfloat16)
    return gather(mine, "y", NY).reshape(steps, seqs, width // groups)


def solution(mesh):
    split = Mesh(mesh.devices.reshape(NY, NZ, -1, 2), ("y", "z", "x", "c"))
    return jax.shard_map(
        local,
        mesh=split,
        in_specs=(
            P(None, None, HEAD, None),
            P(None, CONTEXT, None),
            P(),
            P(),
            P(HEAD, CONTEXT, None),
            P(HEAD, CONTEXT, None),
        ),
        out_specs=P(None, None, HEAD),
        check_vma=False,
    )
```

```python
import math

import jax
import jax.numpy as jnp
from jax import lax
from jax.experimental import pallas as pl
from jax.experimental.pallas import tpu as pltpu
from jax.sharding import Mesh
from jax.sharding import PartitionSpec as P

LAT = 512
ROPE = 64
NY = 4
NZ = 16
LANES = 128

CONTEXT = ("y", "z")
HEAD = ("x", "c")
PLANE = ("y", "x", "c")

score_scale = 192.0 ** (-0.5)
neg_large = -3e38


def exchange(array, axes):
    return lax.all_to_all(array, axes, 0, 0, tiled=True)


def gather(array, axis, size):
    return exchange(jnp.broadcast_to(array[None], (size,) + array.shape), axis)


def swap(blocks, axis):
    size = blocks.shape[0]
    me = lax.axis_index(axis)
    held = []
    for k in range(size):
        block = lax.dynamic_index_in_dim(blocks, me ^ k, 0, keepdims=False)
        if k:
            block = lax.ppermute(block, axis, [(i, i ^ k) for i in range(size)])
        held.append(block)
    return held


def turns(positions, steps, seqs):
    half = ROPE // 2
    shape = (steps * seqs, ROPE)
    row = lax.broadcasted_iota(jnp.int32, shape, 0)
    lane = lax.broadcasted_iota(jnp.int32, shape, 1)
    at = jnp.zeros(shape, jnp.int32)
    for b in range(seqs):
        for s in range(steps):
            at = jnp.where(row == s * seqs + b, positions[b] + s, at)
    freqs = jnp.zeros(shape, jnp.float32)
    for i in range(half):
        freqs = jnp.where(lane % half == i, 10000.0 ** (-2.0 * i / ROPE), freqs)
    angles = at.astype(jnp.float32) * freqs
    rounds = jnp.floor(angles * (0.5 / math.pi) + 0.5)
    high = 6.28125
    middle = 1981.0 / 2**20
    low = 2.0 * math.pi - high - middle
    angles = ((angles - rounds * high) - rounds * middle) - rounds * low
    sine = jnp.sin(angles)
    return jnp.cos(angles), jnp.where(lane < half, -sine, sine)


def attend(queries_hbm, keys_hbm, lengths_hbm, positions_hbm, out_ref,
           queries_ref, keys_ref, lengths_ref, positions_ref, sems):
    steps, seqs, heads, _ = queries_ref.shape
    ctx = keys_ref.shape[2]
    copies = [
        pltpu.make_async_copy(positions_hbm, positions_ref, sems.at[0]),
        pltpu.make_async_copy(lengths_hbm, lengths_ref, sems.at[1]),
        pltpu.make_async_copy(queries_hbm, queries_ref, sems.at[2]),
    ]
    for b in range(seqs):
        copies.append(pltpu.make_async_copy(keys_hbm.at[b], keys_ref.at[b], sems.at[3 + b]))
    for copy in copies:
        copy.start()
    copies[0].wait()
    cosines, sines = turns(positions_ref, steps, seqs)
    copies[2].wait()
    here = lax.axis_index(CONTEXT) * ctx
    place = here + lax.broadcasted_iota(jnp.int32, (heads, ctx), 1)
    near = lax.broadcasted_iota(jnp.int32, (ROPE, ROPE), 0)
    far = lax.broadcasted_iota(jnp.int32, (ROPE, ROPE), 1)
    turn = ((near + ROPE // 2) % ROPE == far).astype(jnp.float32).astype(jnp.bfloat16)
    lane = lax.broadcasted_iota(jnp.int32, (steps * heads, LANES), 1)
    tails = queries_ref[:, :, :, LAT:].reshape(steps * seqs * heads, ROPE)
    others = jnp.dot(tails, turn, preferred_element_type=jnp.float32)
    groups = (steps * seqs, heads, ROPE)
    turned = tails.astype(jnp.float32).reshape(groups) * cosines[:, None, :]
    turned = (turned + others.reshape(groups) * sines[:, None, :]).astype(jnp.bfloat16)
    for copy in copies[1:2] + copies[3:]:
        copy.wait()
    scores = []
    for b in range(seqs):
        plain = jnp.concatenate([queries_ref[s, b, :, :LAT] for s in range(steps)], axis=0)
        tail = jnp.concatenate([turned[s * seqs + b] for s in range(steps)], axis=0)
        both = jnp.dot(plain, keys_ref[b, :LAT], preferred_element_type=jnp.float32)
        both += jnp.dot(tail, keys_ref[b, LAT:], preferred_element_type=jnp.float32)
        scores.append(both * score_scale)
    weights, totals, tops = [], [], []
    for b in range(seqs):
        valid = jnp.concatenate([place < lengths_ref[b] - 1 + s for s in range(steps)], axis=0)
        masked = jnp.where(valid, scores[b], neg_large)
        tops.append(jnp.max(masked, axis=-1, keepdims=True))
        weights.append(jnp.where(valid, jnp.exp(masked - tops[b]), 0.0))
        totals.append(jnp.sum(weights[b], axis=-1, keepdims=True))
    sums = [
        lax.dot_general(
            weights[b].astype(jnp.bfloat16), keys_ref[b, :LAT], (((1,), (1,)), ((), ())),
            preferred_element_type=jnp.float32,
        )
        for b in range(seqs)
    ]
    for b in range(seqs):
        live = totals[b] > 0.0
        total = jnp.where(live, totals[b], 1.0)
        level = jnp.where(live, tops[b] + jnp.log(total), neg_large)
        high = level.astype(jnp.bfloat16).astype(jnp.float32)
        rest = level - high
        middle = rest.astype(jnp.bfloat16).astype(jnp.float32)
        parts = jnp.where(lane == 0, high, jnp.where(lane == 1, middle, rest - middle))
        parts = parts.astype(jnp.bfloat16)
        latents = (sums[b] * (1.0 / total)).astype(jnp.bfloat16)
        for s in range(steps):
            for y in range(NY):
                rows = slice(s * heads + y * (heads // NY), s * heads + (y + 1) * (heads // NY))
                out_ref[y * steps * seqs + s * seqs + b, :, :LAT] = latents[rows]
                out_ref[y * steps * seqs + s * seqs + b, :, LAT:] = parts[rows]


def combine(came_ref, out_ref):
    came = came_ref[:, :, LAT:].astype(jnp.float32)
    levels = came[:, :, 0:1] + came[:, :, 1:2] + came[:, :, 2:3]
    share = jnp.exp(levels - jnp.max(levels, axis=0, keepdims=True))
    share = share / jnp.sum(share, axis=0, keepdims=True)
    latent = jnp.sum(came_ref[:, :, :LAT].astype(jnp.float32) * share, axis=0)
    out_ref[...] = jnp.broadcast_to(latent.astype(jnp.bfloat16)[None], out_ref.shape)


def whole(memory):
    return pl.BlockSpec(memory_space=memory)


def local(queries, cache, lengths, positions, up_weight, out_weight):
    steps, seqs, heads_dev, _ = queries.shape
    width = out_weight.shape[2]
    groups = lax.axis_size("x") * lax.axis_size("c")
    share_heads = heads_dev // NY
    keys = jnp.swapaxes(cache, 1, 2)
    packet = pl.pallas_call(
        attend,
        out_shape=jax.ShapeDtypeStruct((NY * NZ, share_heads, LAT + LANES), jnp.bfloat16),
        in_specs=[whole(pl.ANY)] * 4,
        out_specs=whole(pltpu.VMEM),
        scratch_shapes=[
            pltpu.VMEM(queries.shape, queries.dtype),
            pltpu.VMEM(keys.shape, keys.dtype),
            pltpu.SMEM(lengths.shape, lengths.dtype),
            pltpu.SMEM(positions.shape, positions.dtype),
            pltpu.SemaphoreType.DMA((3 + seqs,)),
        ],
        compiler_params=pltpu.CompilerParams(vmem_limit_bytes=60 * 1024 * 1024),
        cost_estimate=pl.CostEstimate(
            flops=140_000_000, bytes_accessed=3_000_000, transcendentals=70_000
        ),
    )(queries, keys, lengths, positions)
    weights = jnp.concatenate([up_weight, out_weight], axis=-1).reshape(NY, -1, LAT + width)
    weights = swap(weights, "y")
    came, early = lax.optimization_barrier((exchange(packet, CONTEXT), weights[:-2]))
    copies = pl.pallas_call(
        combine,
        out_shape=jax.ShapeDtypeStruct((NZ, share_heads, LAT), jnp.bfloat16),
        in_specs=[whole(pltpu.VMEM)],
        out_specs=whole(pltpu.VMEM),
        compiler_params=pltpu.CompilerParams(vmem_limit_bytes=32 * 1024 * 1024),
        cost_estimate=pl.CostEstimate(
            flops=300_000, bytes_accessed=500_000, transcendentals=300
        ),
    )(came)
    weights = jnp.concatenate(early + weights[-2:], axis=0)
    latent, weights = lax.optimization_barrier((exchange(copies, "z"), weights))
    up, out = weights[:, :LAT], weights[:, LAT:]

    every = jnp.einsum("bhl,kl->bhk", latent, up, preferred_element_type=jnp.float32)
    place = (jnp.arange(up.shape[0], dtype=jnp.int32) // up_weight.shape[1]) % share_heads
    own = place[None, :] == jnp.arange(share_heads, dtype=jnp.int32)[:, None]
    values = jnp.sum(jnp.where(own[None], every, 0.0), axis=1).astype(jnp.bfloat16)
    partial = jnp.dot(values, out, preferred_element_type=jnp.float32).astype(jnp.bfloat16)
    rows = steps * seqs // NY
    partial = partial.reshape(NY, rows, groups, width // groups)
    partial = jnp.transpose(partial, (0, 2, 1, 3)).reshape(NY * groups, rows, width // groups)
    mine = jnp.sum(exchange(partial, PLANE).astype(jnp.float32), axis=0).astype(jnp.bfloat16)
    mine = jnp.sum(gather(mine, "z", NZ).astype(jnp.float32), axis=0).astype(jnp.bfloat16)
    return gather(mine, "y", NY).reshape(steps, seqs, width // groups)


def solution(mesh):
    split = Mesh(mesh.devices.reshape(NY, NZ, -1, 2), ("y", "z", "x", "c"))
    return jax.shard_map(
        local,
        mesh=split,
        in_specs=(
            P(None, None, HEAD, None),
            P(None, CONTEXT, None),
            P(),
            P(),
            P(HEAD, CONTEXT, None),
            P(HEAD, CONTEXT, None),
        ),
        out_specs=P(None, None, HEAD),
        check_vma=False,
    )
```

```python
import math

import jax
import jax.numpy as jnp
from jax import lax
from jax.experimental import pallas as pl
from jax.experimental.pallas import tpu as pltpu
from jax.sharding import Mesh
from jax.sharding import PartitionSpec as P

LAT = 512
ROPE = 64
NY = 4
NZ = 16
LANES = 128

CONTEXT = ("y", "z")
HEAD = ("x", "c")
PLANE = ("y", "x", "c")

score_scale = 192.0 ** (-0.5)
neg_large = -3e38


def exchange(array, axes):
    return lax.all_to_all(array, axes, 0, 0, tiled=True)


def gather(array, axis, size):
    return exchange(jnp.broadcast_to(array[None], (size,) + array.shape), axis)


def swap(blocks, axis):
    size = blocks.shape[0]
    me = lax.axis_index(axis)
    held = []
    for k in range(size):
        block = lax.dynamic_index_in_dim(blocks, me ^ k, 0, keepdims=False)
        if k:
            block = lax.ppermute(block, axis, [(i, i ^ k) for i in range(size)])
        held.append(block)
    return held


def turns(positions, steps, seqs):
    half = ROPE // 2
    shape = (steps * seqs, ROPE)
    row = lax.broadcasted_iota(jnp.int32, shape, 0)
    lane = lax.broadcasted_iota(jnp.int32, shape, 1)
    at = jnp.zeros(shape, jnp.int32)
    for b in range(seqs):
        for s in range(steps):
            at = jnp.where(row == s * seqs + b, positions[b] + s, at)
    freqs = jnp.zeros(shape, jnp.float32)
    for i in range(half):
        freqs = jnp.where(lane % half == i, 10000.0 ** (-2.0 * i / ROPE), freqs)
    angles = at.astype(jnp.float32) * freqs
    rounds = jnp.floor(angles * (0.5 / math.pi) + 0.5)
    high = 6.28125
    middle = 1981.0 / 2**20
    low = 2.0 * math.pi - high - middle
    angles = ((angles - rounds * high) - rounds * middle) - rounds * low
    sine = jnp.sin(angles)
    return jnp.cos(angles), jnp.where(lane < half, -sine, sine)


def attend(queries_hbm, keys_hbm, lengths_hbm, positions_hbm, out_ref,
           queries_ref, keys_ref, lengths_ref, positions_ref, sems):
    steps, seqs, heads, _ = queries_ref.shape
    ctx = keys_ref.shape[2]
    copies = [
        pltpu.make_async_copy(positions_hbm, positions_ref, sems.at[0]),
        pltpu.make_async_copy(lengths_hbm, lengths_ref, sems.at[1]),
        pltpu.make_async_copy(queries_hbm, queries_ref, sems.at[2]),
    ]
    for b in range(seqs):
        copies.append(pltpu.make_async_copy(keys_hbm.at[b], keys_ref.at[b], sems.at[3 + b]))
    for copy in copies:
        copy.start()
    copies[0].wait()
    cosines, sines = turns(positions_ref, steps, seqs)
    copies[2].wait()
    here = lax.axis_index(CONTEXT) * ctx
    place = here + lax.broadcasted_iota(jnp.int32, (heads, ctx), 1)
    near = lax.broadcasted_iota(jnp.int32, (ROPE, ROPE), 0)
    far = lax.broadcasted_iota(jnp.int32, (ROPE, ROPE), 1)
    turn = ((near + ROPE // 2) % ROPE == far).astype(jnp.float32).astype(jnp.bfloat16)
    lane = lax.broadcasted_iota(jnp.int32, (steps * heads, LANES), 1)
    tails = queries_ref[:, :, :, LAT:].reshape(steps * seqs * heads, ROPE)
    others = jnp.dot(tails, turn, preferred_element_type=jnp.float32)
    groups = (steps * seqs, heads, ROPE)
    turned = tails.astype(jnp.float32).reshape(groups) * cosines[:, None, :]
    turned = (turned + others.reshape(groups) * sines[:, None, :]).astype(jnp.bfloat16)
    for copy in copies[1:2] + copies[3:]:
        copy.wait()
    scores = []
    for b in range(seqs):
        plain = jnp.concatenate([queries_ref[s, b, :, :LAT] for s in range(steps)], axis=0)
        tail = jnp.concatenate([turned[s * seqs + b] for s in range(steps)], axis=0)
        both = jnp.dot(plain, keys_ref[b, :LAT], preferred_element_type=jnp.float32)
        both += jnp.dot(tail, keys_ref[b, LAT:], preferred_element_type=jnp.float32)
        scores.append(both * score_scale)
    weights, totals, tops = [], [], []
    for b in range(seqs):
        valid = jnp.concatenate([place < lengths_ref[b] - 1 + s for s in range(steps)], axis=0)
        masked = jnp.where(valid, scores[b], neg_large)
        tops.append(jnp.max(masked, axis=-1, keepdims=True))
        weights.append(jnp.where(valid, jnp.exp(masked - tops[b]), 0.0))
        totals.append(jnp.sum(weights[b], axis=-1, keepdims=True))
    sums = [
        lax.dot_general(
            weights[b].astype(jnp.bfloat16), keys_ref[b, :LAT], (((1,), (1,)), ((), ())),
            preferred_element_type=jnp.float32,
        )
        for b in range(seqs)
    ]
    for b in range(seqs):
        live = totals[b] > 0.0
        total = jnp.where(live, totals[b], 1.0)
        level = jnp.where(live, tops[b] + jnp.log(total), neg_large)
        high = level.astype(jnp.bfloat16).astype(jnp.float32)
        rest = level - high
        middle = rest.astype(jnp.bfloat16).astype(jnp.float32)
        parts = jnp.where(lane == 0, high, jnp.where(lane == 1, middle, rest - middle))
        parts = parts.astype(jnp.bfloat16)
        latents = (sums[b] * (1.0 / total)).astype(jnp.bfloat16)
        for s in range(steps):
            for y in range(NY):
                rows = slice(s * heads + y * (heads // NY), s * heads + (y + 1) * (heads // NY))
                out_ref[y * steps * seqs + s * seqs + b, :, :LAT] = latents[rows]
                out_ref[y * steps * seqs + s * seqs + b, :, LAT:] = parts[rows]


def shares(came_ref):
    parts = came_ref[..., LAT:].astype(jnp.float32)
    levels = parts[..., 0:1] + parts[..., 1:2] + parts[..., 2:3]
    top = jnp.max(levels, axis=0)
    weights = jnp.exp(levels - top[None])
    total = jnp.sum(weights, axis=0)
    return top, total, weights / total[None]


def merge(came_ref, out_ref):
    top, total, share = shares(came_ref)
    latent = jnp.sum(came_ref[..., :LAT].astype(jnp.float32) * share, axis=0)
    out_ref[..., :LAT] = latent.astype(jnp.bfloat16)
    level = top + jnp.log(total)
    high = level.astype(jnp.bfloat16).astype(jnp.float32)
    rest = level - high
    middle = rest.astype(jnp.bfloat16).astype(jnp.float32)
    lane = lax.broadcasted_iota(jnp.int32, out_ref.shape[:-1] + (LANES,), len(out_ref.shape) - 1)
    parts = jnp.where(lane == 0, high, jnp.where(lane == 1, middle, rest - middle))
    out_ref[..., LAT:] = parts.astype(jnp.bfloat16)


def combine(came_ref, out_ref):
    _, _, share = shares(came_ref)
    latent = jnp.sum(came_ref[..., :LAT].astype(jnp.float32) * share, axis=0)
    out_ref[...] = jnp.broadcast_to(latent.astype(jnp.bfloat16)[None], out_ref.shape)


def whole(memory):
    return pl.BlockSpec(memory_space=memory)


def local(queries, cache, lengths, positions, up_weight, out_weight):
    steps, seqs, heads_dev, _ = queries.shape
    width = out_weight.shape[2]
    groups = lax.axis_size("x") * lax.axis_size("c")
    share_heads = heads_dev // NY
    keys = jnp.swapaxes(cache, 1, 2)
    packet = pl.pallas_call(
        attend,
        out_shape=jax.ShapeDtypeStruct((NY * NZ, share_heads, LAT + LANES), jnp.bfloat16),
        in_specs=[whole(pl.ANY)] * 4,
        out_specs=whole(pltpu.VMEM),
        scratch_shapes=[
            pltpu.VMEM(queries.shape, queries.dtype),
            pltpu.VMEM(keys.shape, keys.dtype),
            pltpu.SMEM(lengths.shape, lengths.dtype),
            pltpu.SMEM(positions.shape, positions.dtype),
            pltpu.SemaphoreType.DMA((3 + seqs,)),
        ],
        compiler_params=pltpu.CompilerParams(vmem_limit_bytes=60 * 1024 * 1024),
        cost_estimate=pl.CostEstimate(
            flops=140_000_000, bytes_accessed=3_000_000, transcendentals=70_000
        ),
    )(queries, keys, lengths, positions)
    weights = jnp.concatenate([up_weight, out_weight], axis=-1).reshape(NY, -1, LAT + width)
    weights = swap(weights, "y")
    near = exchange(packet, "y").reshape(NY, NZ, share_heads, LAT + LANES)
    packet = pl.pallas_call(
        merge,
        out_shape=jax.ShapeDtypeStruct((NZ, share_heads, LAT + LANES), jnp.bfloat16),
        in_specs=[whole(pltpu.VMEM)],
        out_specs=whole(pltpu.VMEM),
        compiler_params=pltpu.CompilerParams(vmem_limit_bytes=32 * 1024 * 1024),
        cost_estimate=pl.CostEstimate(
            flops=300_000, bytes_accessed=500_000, transcendentals=400
        ),
    )(near)
    came, early = lax.optimization_barrier((exchange(packet, "z"), weights[:-2]))
    copies = pl.pallas_call(
        combine,
        out_shape=jax.ShapeDtypeStruct((NZ, share_heads, LAT), jnp.bfloat16),
        in_specs=[whole(pltpu.VMEM)],
        out_specs=whole(pltpu.VMEM),
        compiler_params=pltpu.CompilerParams(vmem_limit_bytes=32 * 1024 * 1024),
        cost_estimate=pl.CostEstimate(
            flops=300_000, bytes_accessed=500_000, transcendentals=300
        ),
    )(came)
    weights = jnp.concatenate(early + weights[-2:], axis=0)
    latent, weights = lax.optimization_barrier((exchange(copies, "z"), weights))
    up, out = weights[:, :LAT], weights[:, LAT:]

    every = jnp.einsum("bhl,kl->bhk", latent, up, preferred_element_type=jnp.float32)
    place = (jnp.arange(up.shape[0], dtype=jnp.int32) // up_weight.shape[1]) % share_heads
    own = place[None, :] == jnp.arange(share_heads, dtype=jnp.int32)[:, None]
    values = jnp.sum(jnp.where(own[None], every, 0.0), axis=1).astype(jnp.bfloat16)
    partial = jnp.dot(values, out, preferred_element_type=jnp.float32).astype(jnp.bfloat16)
    rows = steps * seqs // NY
    partial = partial.reshape(NY, rows, groups, width // groups)
    partial = jnp.transpose(partial, (0, 2, 1, 3)).reshape(NY * groups, rows, width // groups)
    mine = jnp.sum(exchange(partial, PLANE).astype(jnp.float32), axis=0).astype(jnp.bfloat16)
    mine = jnp.sum(gather(mine, "z", NZ).astype(jnp.float32), axis=0).astype(jnp.bfloat16)
    return gather(mine, "y", NY).reshape(steps, seqs, width // groups)


def solution(mesh):
    split = Mesh(mesh.devices.reshape(NY, NZ, -1, 2), ("y", "z", "x", "c"))
    return jax.shard_map(
        local,
        mesh=split,
        in_specs=(
            P(None, None, HEAD, None),
            P(None, CONTEXT, None),
            P(),
            P(),
            P(HEAD, CONTEXT, None),
            P(HEAD, CONTEXT, None),
        ),
        out_specs=P(None, None, HEAD),
        check_vma=False,
    )
```

```python
import math

import jax
import jax.numpy as jnp
from jax import lax
from jax.experimental import pallas as pl
from jax.experimental.pallas import tpu as pltpu
from jax.sharding import Mesh
from jax.sharding import PartitionSpec as P

LAT = 512
ROPE = 64
NY = 4
NZ = 16
FIRST = 3
LANES = 128

CONTEXT = ("y", "z")
HEAD = ("x", "c")
PLANE = ("y", "x", "c")

score_scale = 192.0 ** (-0.5)
neg_large = -3e38


def exchange(array, axes):
    return lax.all_to_all(array, axes, 0, 0, tiled=True)


def gather(array, axis, size):
    return exchange(jnp.broadcast_to(array[None], (size,) + array.shape), axis)


def swap(blocks, axis, k):
    size = blocks.shape[0]
    block = lax.dynamic_index_in_dim(blocks, lax.axis_index(axis) ^ k, 0, keepdims=False)
    return lax.ppermute(block, axis, [(i, i ^ k) for i in range(size)]) if k else block


def turns(positions, steps, seqs):
    half = ROPE // 2
    shape = (steps * seqs, ROPE)
    row = lax.broadcasted_iota(jnp.int32, shape, 0)
    lane = lax.broadcasted_iota(jnp.int32, shape, 1)
    at = jnp.zeros(shape, jnp.int32)
    for b in range(seqs):
        for s in range(steps):
            at = jnp.where(row == s * seqs + b, positions[b] + s, at)
    freqs = jnp.zeros(shape, jnp.float32)
    for i in range(half):
        freqs = jnp.where(lane % half == i, 10000.0 ** (-2.0 * i / ROPE), freqs)
    angles = at.astype(jnp.float32) * freqs
    rounds = jnp.floor(angles * (0.5 / math.pi) + 0.5)
    high = 6.28125
    middle = 1981.0 / 2**20
    low = 2.0 * math.pi - high - middle
    angles = ((angles - rounds * high) - rounds * middle) - rounds * low
    sine = jnp.sin(angles)
    return jnp.cos(angles), jnp.where(lane < half, -sine, sine)


def attend(queries_hbm, keys_hbm, lengths_hbm, positions_hbm, out_ref,
           queries_ref, keys_ref, lengths_ref, positions_ref, sems):
    steps, seqs, heads, _ = queries_ref.shape
    ctx = keys_ref.shape[2]
    copies = [
        pltpu.make_async_copy(positions_hbm, positions_ref, sems.at[0]),
        pltpu.make_async_copy(lengths_hbm, lengths_ref, sems.at[1]),
        pltpu.make_async_copy(queries_hbm, queries_ref, sems.at[2]),
    ]
    for b in range(seqs):
        copies.append(pltpu.make_async_copy(keys_hbm.at[b], keys_ref.at[b], sems.at[3 + b]))
    for copy in copies:
        copy.start()
    copies[0].wait()
    cosines, sines = turns(positions_ref, steps, seqs)
    copies[2].wait()
    here = lax.axis_index(CONTEXT) * ctx
    place = here + lax.broadcasted_iota(jnp.int32, (heads, ctx), 1)
    near = lax.broadcasted_iota(jnp.int32, (ROPE, ROPE), 0)
    far = lax.broadcasted_iota(jnp.int32, (ROPE, ROPE), 1)
    turn = ((near + ROPE // 2) % ROPE == far).astype(jnp.float32).astype(jnp.bfloat16)
    lane = lax.broadcasted_iota(jnp.int32, (steps * heads, LANES), 1)
    tails = queries_ref[:, :, :, LAT:].reshape(steps * seqs * heads, ROPE)
    others = jnp.dot(tails, turn, preferred_element_type=jnp.float32)
    groups = (steps * seqs, heads, ROPE)
    turned = tails.astype(jnp.float32).reshape(groups) * cosines[:, None, :]
    turned = (turned + others.reshape(groups) * sines[:, None, :]).astype(jnp.bfloat16)
    for copy in copies[1:2] + copies[3:]:
        copy.wait()
    scores = []
    for b in range(seqs):
        plain = jnp.concatenate([queries_ref[s, b, :, :LAT] for s in range(steps)], axis=0)
        tail = jnp.concatenate([turned[s * seqs + b] for s in range(steps)], axis=0)
        both = jnp.dot(plain, keys_ref[b, :LAT], preferred_element_type=jnp.float32)
        both += jnp.dot(tail, keys_ref[b, LAT:], preferred_element_type=jnp.float32)
        scores.append(both * score_scale)
    weights, totals, tops = [], [], []
    for b in range(seqs):
        valid = jnp.concatenate([place < lengths_ref[b] - 1 + s for s in range(steps)], axis=0)
        masked = jnp.where(valid, scores[b], neg_large)
        tops.append(jnp.max(masked, axis=-1, keepdims=True))
        weights.append(jnp.where(valid, jnp.exp(masked - tops[b]), 0.0))
        totals.append(jnp.sum(weights[b], axis=-1, keepdims=True))
    sums = [
        lax.dot_general(
            weights[b].astype(jnp.bfloat16), keys_ref[b, :LAT], (((1,), (1,)), ((), ())),
            preferred_element_type=jnp.float32,
        )
        for b in range(seqs)
    ]
    for b in range(seqs):
        live = totals[b] > 0.0
        total = jnp.where(live, totals[b], 1.0)
        level = jnp.where(live, tops[b] + jnp.log(total), neg_large)
        high = level.astype(jnp.bfloat16).astype(jnp.float32)
        rest = level - high
        middle = rest.astype(jnp.bfloat16).astype(jnp.float32)
        parts = jnp.where(lane == 0, high, jnp.where(lane == 1, middle, rest - middle))
        parts = parts.astype(jnp.bfloat16)
        latents = (sums[b] * (1.0 / total)).astype(jnp.bfloat16)
        for s in range(steps):
            for y in range(NY):
                rows = slice(s * heads + y * (heads // NY), s * heads + (y + 1) * (heads // NY))
                out_ref[y * steps * seqs + s * seqs + b, :, :LAT] = latents[rows]
                out_ref[y * steps * seqs + s * seqs + b, :, LAT:] = parts[rows]


def shares(came_ref):
    parts = came_ref[..., LAT:].astype(jnp.float32)
    levels = parts[..., 0:1] + parts[..., 1:2] + parts[..., 2:3]
    top = jnp.max(levels, axis=0)
    weights = jnp.exp(levels - top[None])
    total = jnp.sum(weights, axis=0)
    return top, total, weights / total[None]


def merge(came_ref, out_ref):
    top, total, share = shares(came_ref)
    latent = jnp.sum(came_ref[..., :LAT].astype(jnp.float32) * share, axis=0)
    out_ref[..., :LAT] = latent.astype(jnp.bfloat16)
    level = top + jnp.log(total)
    high = level.astype(jnp.bfloat16).astype(jnp.float32)
    rest = level - high
    middle = rest.astype(jnp.bfloat16).astype(jnp.float32)
    lane = lax.broadcasted_iota(jnp.int32, out_ref.shape[:-1] + (LANES,), len(out_ref.shape) - 1)
    parts = jnp.where(lane == 0, high, jnp.where(lane == 1, middle, rest - middle))
    out_ref[..., LAT:] = parts.astype(jnp.bfloat16)


def combine(came_ref, out_ref):
    _, _, share = shares(came_ref)
    latent = jnp.sum(came_ref[..., :LAT].astype(jnp.float32) * share, axis=0)
    out_ref[...] = jnp.broadcast_to(latent.astype(jnp.bfloat16)[None], out_ref.shape)


def whole(memory):
    return pl.BlockSpec(memory_space=memory)


def local(queries, cache, lengths, positions, up_weight, out_weight):
    steps, seqs, heads_dev, _ = queries.shape
    width = out_weight.shape[2]
    groups = lax.axis_size("x") * lax.axis_size("c")
    share_heads = heads_dev // NY
    keys = jnp.swapaxes(cache, 1, 2)
    packet = pl.pallas_call(
        attend,
        out_shape=jax.ShapeDtypeStruct((NY * NZ, share_heads, LAT + LANES), jnp.bfloat16),
        in_specs=[whole(pl.ANY)] * 4,
        out_specs=whole(pltpu.VMEM),
        scratch_shapes=[
            pltpu.VMEM(queries.shape, queries.dtype),
            pltpu.VMEM(keys.shape, keys.dtype),
            pltpu.SMEM(lengths.shape, lengths.dtype),
            pltpu.SMEM(positions.shape, positions.dtype),
            pltpu.SemaphoreType.DMA((3 + seqs,)),
        ],
        compiler_params=pltpu.CompilerParams(vmem_limit_bytes=60 * 1024 * 1024),
        cost_estimate=pl.CostEstimate(
            flops=140_000_000, bytes_accessed=3_000_000, transcendentals=70_000
        ),
    )(queries, keys, lengths, positions)
    weights = jnp.concatenate([up_weight, out_weight], axis=-1).reshape(NY, -1, LAT + width)
    first = [swap(weights, "y", k) for k in range(FIRST)]
    near = exchange(packet, "y").reshape(NY, NZ, share_heads, LAT + LANES)
    packet = pl.pallas_call(
        merge,
        out_shape=jax.ShapeDtypeStruct((NZ, share_heads, LAT + LANES), jnp.bfloat16),
        in_specs=[whole(pltpu.VMEM)],
        out_specs=whole(pltpu.VMEM),
        compiler_params=pltpu.CompilerParams(vmem_limit_bytes=32 * 1024 * 1024),
        cost_estimate=pl.CostEstimate(
            flops=300_000, bytes_accessed=500_000, transcendentals=400
        ),
    )(near)
    packet, weights = lax.optimization_barrier((packet, weights))
    later = [swap(weights, "y", k) for k in range(FIRST, NY)]
    came, first = lax.optimization_barrier((exchange(packet, "z"), first))
    copies = pl.pallas_call(
        combine,
        out_shape=jax.ShapeDtypeStruct((NZ, share_heads, LAT), jnp.bfloat16),
        in_specs=[whole(pltpu.VMEM)],
        out_specs=whole(pltpu.VMEM),
        compiler_params=pltpu.CompilerParams(vmem_limit_bytes=32 * 1024 * 1024),
        cost_estimate=pl.CostEstimate(
            flops=300_000, bytes_accessed=500_000, transcendentals=300
        ),
    )(came)
    weights = jnp.concatenate(first + later, axis=0)
    latent, weights = lax.optimization_barrier((exchange(copies, "z"), weights))
    up, out = weights[:, :LAT], weights[:, LAT:]

    every = jnp.einsum("bhl,kl->bhk", latent, up, preferred_element_type=jnp.float32)
    place = (jnp.arange(up.shape[0], dtype=jnp.int32) // up_weight.shape[1]) % share_heads
    own = place[None, :] == jnp.arange(share_heads, dtype=jnp.int32)[:, None]
    values = jnp.sum(jnp.where(own[None], every, 0.0), axis=1).astype(jnp.bfloat16)
    partial = jnp.dot(values, out, preferred_element_type=jnp.float32).astype(jnp.bfloat16)
    rows = steps * seqs // NY
    partial = partial.reshape(NY, rows, groups, width // groups)
    partial = jnp.transpose(partial, (0, 2, 1, 3)).reshape(NY * groups, rows, width // groups)
    mine = jnp.sum(exchange(partial, PLANE).astype(jnp.float32), axis=0).astype(jnp.bfloat16)
    mine = jnp.sum(gather(mine, "z", NZ).astype(jnp.float32), axis=0).astype(jnp.bfloat16)
    return gather(mine, "y", NY).reshape(steps, seqs, width // groups)


def solution(mesh):
    split = Mesh(mesh.devices.reshape(NY, NZ, -1, 2), ("y", "z", "x", "c"))
    return jax.shard_map(
        local,
        mesh=split,
        in_specs=(
            P(None, None, HEAD, None),
            P(None, CONTEXT, None),
            P(),
            P(),
            P(HEAD, CONTEXT, None),
            P(HEAD, CONTEXT, None),
        ),
        out_specs=P(None, None, HEAD),
        check_vma=False,
    )
```

```python
import math

import jax
import jax.numpy as jnp
from jax import lax
from jax.experimental import pallas as pl
from jax.experimental.pallas import tpu as pltpu
from jax.sharding import Mesh
from jax.sharding import PartitionSpec as P

LAT = 512
ROPE = 64
NY = 4
NZ = 16
FIRST = 2
LANES = 128

CONTEXT = ("y", "z")
HEAD = ("x", "c")
PLANE = ("y", "x", "c")

score_scale = 192.0 ** (-0.5)
neg_large = -3e38


def exchange(array, axes):
    return lax.all_to_all(array, axes, 0, 0, tiled=True)


def gather(array, axis, size):
    return exchange(jnp.broadcast_to(array[None], (size,) + array.shape), axis)


def swap(blocks, axis, k):
    size = blocks.shape[0]
    block = lax.dynamic_index_in_dim(blocks, lax.axis_index(axis) ^ k, 0, keepdims=False)
    return lax.ppermute(block, axis, [(i, i ^ k) for i in range(size)]) if k else block


def turns(positions, steps, seqs):
    half = ROPE // 2
    shape = (steps * seqs, ROPE)
    row = lax.broadcasted_iota(jnp.int32, shape, 0)
    lane = lax.broadcasted_iota(jnp.int32, shape, 1)
    at = jnp.zeros(shape, jnp.int32)
    for b in range(seqs):
        for s in range(steps):
            at = jnp.where(row == s * seqs + b, positions[b] + s, at)
    freqs = jnp.zeros(shape, jnp.float32)
    for i in range(half):
        freqs = jnp.where(lane % half == i, 10000.0 ** (-2.0 * i / ROPE), freqs)
    angles = at.astype(jnp.float32) * freqs
    rounds = jnp.floor(angles * (0.5 / math.pi) + 0.5)
    high = 6.28125
    middle = 1981.0 / 2**20
    low = 2.0 * math.pi - high - middle
    angles = ((angles - rounds * high) - rounds * middle) - rounds * low
    sine = jnp.sin(angles)
    return jnp.cos(angles), jnp.where(lane < half, -sine, sine)


def attend(queries_hbm, keys_hbm, lengths_hbm, positions_hbm, out_ref,
           queries_ref, keys_ref, lengths_ref, positions_ref, sems):
    steps, seqs, heads, _ = queries_ref.shape
    ctx = keys_ref.shape[2]
    copies = [
        pltpu.make_async_copy(positions_hbm, positions_ref, sems.at[0]),
        pltpu.make_async_copy(lengths_hbm, lengths_ref, sems.at[1]),
        pltpu.make_async_copy(queries_hbm, queries_ref, sems.at[2]),
    ]
    for b in range(seqs):
        copies.append(pltpu.make_async_copy(keys_hbm.at[b], keys_ref.at[b], sems.at[3 + b]))
    for copy in copies:
        copy.start()
    copies[0].wait()
    cosines, sines = turns(positions_ref, steps, seqs)
    copies[2].wait()
    here = lax.axis_index(CONTEXT) * ctx
    place = here + lax.broadcasted_iota(jnp.int32, (heads, ctx), 1)
    near = lax.broadcasted_iota(jnp.int32, (ROPE, ROPE), 0)
    far = lax.broadcasted_iota(jnp.int32, (ROPE, ROPE), 1)
    turn = ((near + ROPE // 2) % ROPE == far).astype(jnp.float32).astype(jnp.bfloat16)
    lane = lax.broadcasted_iota(jnp.int32, (steps * heads, LANES), 1)
    tails = queries_ref[:, :, :, LAT:].reshape(steps * seqs * heads, ROPE)
    others = jnp.dot(tails, turn, preferred_element_type=jnp.float32)
    groups = (steps * seqs, heads, ROPE)
    turned = tails.astype(jnp.float32).reshape(groups) * cosines[:, None, :]
    turned = (turned + others.reshape(groups) * sines[:, None, :]).astype(jnp.bfloat16)
    for copy in copies[1:2] + copies[3:]:
        copy.wait()
    scores = []
    for b in range(seqs):
        plain = jnp.concatenate([queries_ref[s, b, :, :LAT] for s in range(steps)], axis=0)
        tail = jnp.concatenate([turned[s * seqs + b] for s in range(steps)], axis=0)
        both = jnp.dot(plain, keys_ref[b, :LAT], preferred_element_type=jnp.float32)
        both += jnp.dot(tail, keys_ref[b, LAT:], preferred_element_type=jnp.float32)
        scores.append(both * score_scale)
    weights, totals, tops = [], [], []
    for b in range(seqs):
        valid = jnp.concatenate([place < lengths_ref[b] - 1 + s for s in range(steps)], axis=0)
        masked = jnp.where(valid, scores[b], neg_large)
        tops.append(jnp.max(masked, axis=-1, keepdims=True))
        weights.append(jnp.where(valid, jnp.exp(masked - tops[b]), 0.0))
        totals.append(jnp.sum(weights[b], axis=-1, keepdims=True))
    sums = [
        lax.dot_general(
            weights[b].astype(jnp.bfloat16), keys_ref[b, :LAT], (((1,), (1,)), ((), ())),
            preferred_element_type=jnp.float32,
        )
        for b in range(seqs)
    ]
    for b in range(seqs):
        live = totals[b] > 0.0
        total = jnp.where(live, totals[b], 1.0)
        level = jnp.where(live, tops[b] + jnp.log(total), neg_large)
        high = level.astype(jnp.bfloat16).astype(jnp.float32)
        rest = level - high
        middle = rest.astype(jnp.bfloat16).astype(jnp.float32)
        parts = jnp.where(lane == 0, high, jnp.where(lane == 1, middle, rest - middle))
        parts = parts.astype(jnp.bfloat16)
        latents = (sums[b] * (1.0 / total)).astype(jnp.bfloat16)
        for s in range(steps):
            for y in range(NY):
                rows = slice(s * heads + y * (heads // NY), s * heads + (y + 1) * (heads // NY))
                out_ref[y * steps * seqs + s * seqs + b, :, :LAT] = latents[rows]
                out_ref[y * steps * seqs + s * seqs + b, :, LAT:] = parts[rows]


def shares(came_ref):
    parts = came_ref[..., LAT:].astype(jnp.float32)
    levels = parts[..., 0:1] + parts[..., 1:2] + parts[..., 2:3]
    top = jnp.max(levels, axis=0)
    weights = jnp.exp(levels - top[None])
    total = jnp.sum(weights, axis=0)
    return top, total, weights / total[None]


def merge(came_ref, out_ref):
    top, total, share = shares(came_ref)
    latent = jnp.sum(came_ref[..., :LAT].astype(jnp.float32) * share, axis=0)
    out_ref[..., :LAT] = latent.astype(jnp.bfloat16)
    level = top + jnp.log(total)
    high = level.astype(jnp.bfloat16).astype(jnp.float32)
    rest = level - high
    middle = rest.astype(jnp.bfloat16).astype(jnp.float32)
    lane = lax.broadcasted_iota(jnp.int32, out_ref.shape[:-1] + (LANES,), len(out_ref.shape) - 1)
    parts = jnp.where(lane == 0, high, jnp.where(lane == 1, middle, rest - middle))
    out_ref[..., LAT:] = parts.astype(jnp.bfloat16)


def combine(came_ref, out_ref):
    _, _, share = shares(came_ref)
    latent = jnp.sum(came_ref[..., :LAT].astype(jnp.float32) * share, axis=0)
    out_ref[...] = jnp.broadcast_to(latent.astype(jnp.bfloat16)[None], out_ref.shape)


def whole(memory):
    return pl.BlockSpec(memory_space=memory)


def local(queries, cache, lengths, positions, up_weight, out_weight):
    steps, seqs, heads_dev, _ = queries.shape
    width = out_weight.shape[2]
    groups = lax.axis_size("x") * lax.axis_size("c")
    share_heads = heads_dev // NY
    keys = jnp.swapaxes(cache, 1, 2)
    packet = pl.pallas_call(
        attend,
        out_shape=jax.ShapeDtypeStruct((NY * NZ, share_heads, LAT + LANES), jnp.bfloat16),
        in_specs=[whole(pl.ANY)] * 4,
        out_specs=whole(pltpu.VMEM),
        scratch_shapes=[
            pltpu.VMEM(queries.shape, queries.dtype),
            pltpu.VMEM(keys.shape, keys.dtype),
            pltpu.SMEM(lengths.shape, lengths.dtype),
            pltpu.SMEM(positions.shape, positions.dtype),
            pltpu.SemaphoreType.DMA((3 + seqs,)),
        ],
        compiler_params=pltpu.CompilerParams(vmem_limit_bytes=60 * 1024 * 1024),
        cost_estimate=pl.CostEstimate(
            flops=140_000_000, bytes_accessed=3_000_000, transcendentals=70_000
        ),
    )(queries, keys, lengths, positions)
    weights = jnp.concatenate([up_weight, out_weight], axis=-1).reshape(NY, -1, LAT + width)
    first = [swap(weights, "y", k) for k in range(FIRST)]
    near = exchange(packet, "y").reshape(NY, NZ, share_heads, LAT + LANES)
    packet = pl.pallas_call(
        merge,
        out_shape=jax.ShapeDtypeStruct((NZ, share_heads, LAT + LANES), jnp.bfloat16),
        in_specs=[whole(pltpu.VMEM)],
        out_specs=whole(pltpu.VMEM),
        compiler_params=pltpu.CompilerParams(vmem_limit_bytes=32 * 1024 * 1024),
        cost_estimate=pl.CostEstimate(
            flops=300_000, bytes_accessed=500_000, transcendentals=400
        ),
    )(near)
    packet, weights = lax.optimization_barrier((packet, weights))
    later = [swap(weights, "y", k) for k in range(FIRST, NY)]
    came, first = lax.optimization_barrier((exchange(packet, "z"), first))
    copies = pl.pallas_call(
        combine,
        out_shape=jax.ShapeDtypeStruct((NZ, share_heads, LAT), jnp.bfloat16),
        in_specs=[whole(pltpu.VMEM)],
        out_specs=whole(pltpu.VMEM),
        compiler_params=pltpu.CompilerParams(vmem_limit_bytes=32 * 1024 * 1024),
        cost_estimate=pl.CostEstimate(
            flops=300_000, bytes_accessed=500_000, transcendentals=300
        ),
    )(came)
    weights = jnp.concatenate(first + later, axis=0)
    latent, weights = lax.optimization_barrier((exchange(copies, "z"), weights))
    up, out = weights[:, :LAT], weights[:, LAT:]

    every = jnp.einsum("bhl,kl->bhk", latent, up, preferred_element_type=jnp.float32)
    place = (jnp.arange(up.shape[0], dtype=jnp.int32) // up_weight.shape[1]) % share_heads
    own = place[None, :] == jnp.arange(share_heads, dtype=jnp.int32)[:, None]
    values = jnp.sum(jnp.where(own[None], every, 0.0), axis=1).astype(jnp.bfloat16)
    partial = jnp.dot(values, out, preferred_element_type=jnp.float32).astype(jnp.bfloat16)
    rows = steps * seqs // NY
    partial = partial.reshape(NY, rows, groups, width // groups)
    partial = jnp.transpose(partial, (0, 2, 1, 3)).reshape(NY * groups, rows, width // groups)
    mine = jnp.sum(exchange(partial, PLANE).astype(jnp.float32), axis=0).astype(jnp.bfloat16)
    mine = jnp.sum(gather(mine, "z", NZ).astype(jnp.float32), axis=0).astype(jnp.bfloat16)
    return gather(mine, "y", NY).reshape(steps, seqs, width // groups)


def solution(mesh):
    split = Mesh(mesh.devices.reshape(NY, NZ, -1, 2), ("y", "z", "x", "c"))
    return jax.shard_map(
        local,
        mesh=split,
        in_specs=(
            P(None, None, HEAD, None),
            P(None, CONTEXT, None),
            P(),
            P(),
            P(HEAD, CONTEXT, None),
            P(HEAD, CONTEXT, None),
        ),
        out_specs=P(None, None, HEAD),
        check_vma=False,
    )
```
